512 devices in a mesh: member: 64 (over x, z), space: 8 (over y, core).
Axes of the slice: x: 4, y: 4, z: 16, core: 2. Of those that a mesh axis runs over, the one named last changes fastest.
Arguments:
- replica_profiles: float32 [64, 4, 65536], P('member', None, 'space'), may hold values from -6 to 6
- diffusion: float32 [4], replicated, may hold values from 0.04 to 0.16
- velocity: float32 [3, 4], replicated, may hold values from -0.3 to 0.3
- detector_voxel_position: int32 [20480], P(('member', 'space')), may hold values from 14 to 65535, as said below
- detector_quantity_choice: int32 [20480], P(('member', 'space')), may hold values from 0 to 3
- sensor_value: float32 [20480], P(('member', 'space')), may hold values from -48 to 48
- sensor_var: float32 [20480], P(('member', 'space')), may hold values from 80 to 1280
Outputs:
- analysis: float32 [64, 4, 65536], P('member', None, 'space')
The draws below stay inside these ranges and needn't reach their ends.
Inputs may be any that keep to these rules, and one draw needn't show every extreme that they name: `detector_voxel_position`: A sensor held by the device with member index i and space index j lies in one of the two top layers (z = 14 or 15) of the cells j * 8192 + i * 128 to j * 8192 + i * 128 + 127.
All inputs are finite; a program needn't handle non-finite values.
Results may differ from the reference program's by a relative error of at most 0.00014.
Values sent between devices are 32-bit elements; how exact they have to be, the bound alone decides.
No kernel may reach another device: no remote copies, remote signals or barrier semaphores. Data moves between devices by JAX's collectives and lax.ppermute only.
A program may use at most 64 MiB of HBM per device.

```python
import math
import jax
import jax.numpy as jnp
from jax import lax

F = 4
NY = 256
NZ = 16
OBS_DEV = 40
NS_ITERS = 5
M = 64
NX = 16
CELLS_DEV = 8192
CELLS = 65536
GROUP = 128
SENSORS = 20480
N_MEMBER = 64
N_SPACE = 8


def draw_detector_voxel_position(key, part):
    key = jax.random.fold_in(key, 11)
    first_key, second_key = jax.random.split(key)
    sensors_all = OBS_DEV * N_MEMBER * N_SPACE
    position = jnp.arange(sensors_all, dtype=jnp.int32)
    owner = position // OBS_DEV
    within = position % OBS_DEV
    member_index = owner // N_SPACE
    space_index = owner % N_SPACE
    block_start = space_index * CELLS_DEV + member_index * GROUP
    columns = GROUP // NZ
    column = jax.random.randint(first_key, (sensors_all,), 0, columns, dtype=jnp.int32)
    layer = jax.random.randint(second_key, (sensors_all,), 0, 2, dtype=jnp.int32)
    column = jnp.where(within == 0, 0, jnp.where(within == OBS_DEV - 1, columns - 1, column))
    layer = jnp.where(within == 0, 0, jnp.where(within == OBS_DEV - 1, 1, layer))
    return (block_start + column * NZ + NZ - 2 + layer).astype(jnp.int32)


def with_ends(result, own_key, low, largest):
    dims = result.shape
    index_at = [jax.random.randint(jax.random.fold_in(own_key, axis), (), 0, dims[axis]) for axis in range(len(dims))]
    result = result.at[tuple(index_at)].set(low)
    longest = dims.index(max(dims))
    index_at[longest] = (index_at[longest] + 1) % dims[longest]
    return result.at[tuple(index_at)].set(largest)


def block_levels(own_key, extent, pieces, low, high):
    gain, own = 1.0, jax.random.fold_in(own_key, 6)
    for axis_at, blocks in pieces:
        steps = jnp.exp(jax.random.uniform(jax.random.fold_in(own, axis_at), (blocks,), jnp.float32, low / len(pieces), high / len(pieces)))
        gain = gain * jnp.repeat(steps, extent[axis_at] // blocks).reshape([-1 if axis == axis_at else 1 for axis in range(len(extent))])
    return gain


def gaussian(rng, shape, scale, most, cuts=(), kind=jnp.bfloat16):
    level = block_levels(rng, shape, cuts, -0.22, 0.18) if cuts else 1.0
    values = jax.random.normal(rng, shape, jnp.float32) * scale * level
    return jnp.minimum(jnp.maximum(values, -most), most).astype(kind)


def setup_inputs(seed: int = 0) -> dict:
    splits = jax.random.split(jax.random.key(seed), 8)
    return {
        "replica_profiles": gaussian(splits[0], (M, F, CELLS), 1.0, 6.0, ((0, 64), (2, 8)), jnp.float32),
        "diffusion": jnp.clip(jnp.exp(jax.random.uniform(splits[1], (F,), jnp.float32, math.log(0.04), math.log(0.16))), 0.04, 0.16),
        "velocity": jnp.clip(jax.random.uniform(splits[2], (3, F), jnp.float32, -0.3, 0.3), -0.3, 0.3),
        "detector_voxel_position": draw_detector_voxel_position(jax.random.fold_in(splits[7], 71), 0),
        "detector_quantity_choice": with_ends(jax.random.randint(splits[4], (SENSORS,), 0, F), jax.random.fold_in(splits[4], 1), 0, F - 1).astype(jnp.int32),
        "sensor_value": gaussian(splits[5], (SENSORS,), 8.0, 48.0, ((0, 512),), jnp.float32),
        "sensor_var": jnp.clip(jnp.exp(math.log(1280.0) - 2.7725887 * jax.random.uniform(splits[6], (SENSORS,), jnp.float32) ** block_levels(splits[6], (SENSORS,), ((0, 512),), -0.2, 0.2)), 80.0, 1280.0),
    }


precise_mode = lax.Precision.HIGHEST

def tendency(centre, forward_x, behind_x, forward_y, behind_y, forward_z, behind_z, diffusion, velocity):
    laplace = forward_x + behind_x - 2.0 * centre + (forward_y + behind_y - 2.0 * centre) + (forward_z + behind_z - 2.0 * centre)
    transport = velocity[0] * (forward_x - behind_x) + velocity[1] * (forward_y - behind_y) + velocity[2] * (forward_z - behind_z)
    return centre + diffusion * laplace - 0.5 * transport

def advance(present_quantity, diffusion, velocity):
    padded = jnp.pad(present_quantity, ((0, 0), (1, 1), (1, 1), (1, 1)))
    centre = padded[:, 1:-1, 1:-1, 1:-1]
    return tendency(centre, padded[:, 2:, 1:-1, 1:-1], padded[:, :-2, 1:-1, 1:-1], padded[:, 1:-1, 2:, 1:-1], padded[:, 1:-1, :-2, 1:-1], padded[:, 1:-1, 1:-1, 2:], padded[:, 1:-1, 1:-1, :-2], diffusion, velocity)

def statistics(random_picks, sensor_value, sensor_var):
    sample_mean = lax.optimization_barrier(jnp.mean(random_picks, axis=0))
    deviation = random_picks - sample_mean
    innovation = sensor_value - sample_mean
    weight = 1.0 / sensor_var
    inner_product_table = jnp.dot(deviation * weight, deviation.T, precision=precise_mode, preferred_element_type=jnp.float32)
    anomaly_outer_term = jnp.dot(deviation, weight * innovation, precision=precise_mode, preferred_element_type=jnp.float32)
    return (inner_product_table, anomaly_outer_term)

def analysis_mixing_coefficients(inner_product_table, anomaly_outer_term):
    members = inner_product_table.shape[0]
    identity = jnp.eye(members, dtype=jnp.float32)
    system = (members - 1.0) * identity + inner_product_table
    scale = jnp.sqrt(jnp.sum(system * system))

    def iterate(counter, carry):
        root, inverse_root = carry
        factor = 0.5 * (3.0 * identity - jnp.dot(inverse_root, root, precision=precise_mode))
        return (jnp.dot(root, factor, precision=precise_mode), jnp.dot(factor, inverse_root, precision=precise_mode))
    root, inverse_root = lax.fori_loop(0, NS_ITERS, iterate, (system / scale, identity))
    inverse = jnp.dot(inverse_root, inverse_root, precision=precise_mode) / scale
    shift_weights = jnp.dot(inverse, anomaly_outer_term, precision=precise_mode)
    return jnp.sqrt(members - 1.0) * inverse_root / jnp.sqrt(scale) + shift_weights[:, None]

def correct_replicas(member_ensemble, weights):
    centre = lax.optimization_barrier(jnp.mean(member_ensemble, axis=0))
    anomaly = member_ensemble - centre
    return centre + jnp.einsum('kfc,km->mfc', anomaly, weights, precision=precise_mode)

def reference(replica_profiles, diffusion, velocity, detector_voxel_position, detector_quantity_choice, sensor_value, sensor_var):
    diffuse = diffusion[:, None, None, None]
    moving = velocity[:, :, None, None, None]

    def predict_one_replica(replica_state_array):
        present_quantity = replica_state_array.reshape(F, NX, NY, NZ)
        present_quantity = advance(advance(present_quantity, diffuse, moving), diffuse, moving)
        return present_quantity.reshape(F, NX * NY * NZ)
    predict_replicas = lax.map(predict_one_replica, replica_profiles)
    random_picks = predict_replicas[:, detector_quantity_choice, detector_voxel_position]
    inner_product_table, anomaly_outer_term = statistics(random_picks, sensor_value, sensor_var)
    return correct_replicas(predict_replicas, analysis_mixing_coefficients(inner_product_table, anomaly_outer_term))
```

```python
import functools
import math

import jax
import jax.numpy as jnp
from jax import lax
from jax.experimental import pallas as pl
from jax.experimental.pallas import tpu as pltpu
from jax.sharding import Mesh, PartitionSpec as P

F = 4
NY = 256
NZ = 16
NS_ITERS = 5
MX = 4
MZ = 16
SIDES = 2
MEMBERS = MX * MZ
LANES = 128
PLANE = NY * NZ
CHUNKS = PLANE // LANES
FLAT = 8 * CHUNKS
SUMS = 8 * 7
FLOPS = 10**8
MESSAGE = 2 * F + 1
TABLE = MEMBERS * MEMBERS // 2 // LANES + 1

VMEM = pl.BlockSpec(memory_space=pltpu.VMEM)
SMEM = pl.BlockSpec(memory_space=pltpu.SMEM)
F32 = jnp.float32
MEMBER = ("mx", "mz", "side")
SPACE = ("y", "core")


def call(body, out_shape, in_specs, *operands, flops=None):
    return pl.pallas_call(
        body,
        out_shape=jax.ShapeDtypeStruct(out_shape, F32),
        in_specs=in_specs,
        out_specs=VMEM,
        cost_estimate=flops
        and pl.CostEstimate(flops=flops, bytes_accessed=1 << 18, transcendentals=0),
        compiler_params=pltpu.CompilerParams(vmem_limit_bytes=16 << 20),
    )(*operands)


def in_plane(centre, coef):
    keep, y_next, y_prev, z_next, z_prev = coef
    lane = lax.broadcasted_iota(jnp.int32, centre[0].shape, 1)
    up = [pltpu.roll(tile, LANES - NZ, 1) for tile in centre]
    down = [pltpu.roll(tile, NZ, 1) for tile in centre]
    zero = jnp.zeros_like(centre[0])
    result = []
    for j in range(CHUNKS):
        after = up[j + 1] if j + 1 < CHUNKS else zero
        before = down[j - 1] if j > 0 else zero
        result.append(
            keep * centre[j]
            + y_next * jnp.where(lane < LANES - NZ, up[j], after)
            + y_prev * jnp.where(lane >= NZ, down[j], before)
            + z_next * pltpu.roll(centre[j], LANES - 1, 1)
            + z_prev * pltpu.roll(centre[j], 1, 1)
        )
    return result


def stack(low, high):
    return jnp.concatenate([low, high], axis=0)


def sensor_sums(cell, choice, value, var):
    count = cell.shape[1]
    diagonal = lax.broadcasted_iota(jnp.int32, (count, count), 0) == lax.broadcasted_iota(
        jnp.int32, (count, count), 1
    )

    def column(row):
        return jnp.sum(jnp.where(diagonal, row, 0.0), axis=1, keepdims=True)

    weight = 1.0 / var
    spot = column((cell - 14 + 2 * choice).astype(F32)).astype(jnp.int32)
    lane = lax.broadcasted_iota(jnp.int32, (count, LANES), 1)
    share = jnp.where(spot == lane, column(weight), 0.0)
    share = share + jnp.where(spot + 2 * F == lane, column(weight * value), 0.0)
    return jnp.sum(share, axis=0, keepdims=True)


def early_body(diffusion_ref, velocity_ref, position_ref, choice_ref, value_ref, var_ref, out_ref):
    shape = (2 * F, LANES)
    field = lax.broadcasted_iota(jnp.int32, shape, 0) % F
    inner_z = lax.broadcasted_iota(jnp.int32, shape, 1) % NZ

    def per_field(values):
        tile = jnp.full(shape, values[F - 1], F32)
        for f in range(F - 1):
            tile = jnp.where(field == f, values[f], tile)
        return tile

    diffuse = per_field([diffusion_ref[f] for f in range(F)])
    move = [per_field([0.5 * velocity_ref[a, f] for f in range(F)]) for a in range(3)]
    coef = (
        1.0 - 6.0 * diffuse,
        diffuse - move[1],
        diffuse + move[1],
        jnp.where(inner_z != NZ - 1, diffuse - move[2], 0.0),
        jnp.where(inner_z != 0, diffuse + move[2], 0.0),
        diffuse - move[0],
        diffuse + move[0],
    )
    for i in range(len(coef)):
        out_ref[8 * i : 8 * i + 8, :] = coef[i]
    start = lax.axis_index(SPACE) * (2 * PLANE) + lax.axis_index(MEMBER) * LANES
    out_ref[SUMS : SUMS + 8, :] = jnp.broadcast_to(
        sensor_sums(position_ref[...] - start, choice_ref[...], value_ref[...], var_ref[...]), shape
    )


def own_body(early_ref, own_ref, out_ref):
    own = [stack(own_ref[:, tile(0, j)], own_ref[:, tile(1, j)]) for j in range(CHUNKS)]
    flat = in_plane(own, [early_ref[8 * i : 8 * i + 8, :] for i in range(5)])
    for j in range(CHUNKS):
        out_ref[8 * j : 8 * j + 8, :] = own[j]
        out_ref[FLAT + 8 * j : FLAT + 8 * j + 8, :] = flat[j]


def tile(plane, chunk):
    return slice(plane * PLANE + chunk * LANES, plane * PLANE + (chunk + 1) * LANES)


def forecast_body(early_ref, own_ref, beside_ref, across_ref, out_ref):
    slab = lax.axis_index(SPACE)
    even = slab % 2 == 0
    coef = [early_ref[8 * i : 8 * i + 8, :] for i in range(7)]
    x_next, x_prev = coef[5:]
    own = [own_ref[8 * j : 8 * j + 8, :] for j in range(CHUNKS)]

    def neighbour(first_ref, second_ref, plane, j):
        return jnp.where(even, first_ref[:, tile(plane, j)], second_ref[:, tile(plane, j)])

    left = [[neighbour(across_ref, beside_ref, p, j) for j in range(CHUNKS)] for p in range(2)]
    right = [[neighbour(beside_ref, across_ref, p, j) for j in range(CHUNKS)] for p in range(2)]
    upper = lax.broadcasted_iota(jnp.int32, (2 * F, LANES), 0) >= F
    inside = jnp.where(
        upper,
        jnp.where(slab < lax.axis_size(SPACE) - 1, 1.0, 0.0),
        jnp.where(slab > 0, 1.0, 0.0),
    )
    halo = [stack(left[1][j], right[0][j]) for j in range(CHUNKS)]
    halo_flat = in_plane(halo, coef[:5])
    outer = [
        inside
        * (
            halo_flat[j]
            + x_next * stack(own[j][:F], right[1][j])
            + x_prev * stack(left[0][j], own[j][F:])
        )
        for j in range(CHUNKS)
    ]
    inner = [
        own_ref[FLAT + 8 * j : FLAT + 8 * j + 8, :]
        + x_next * stack(own[j][F:], halo[j][F:])
        + x_prev * stack(halo[j][:F], own[j][:F])
        for j in range(CHUNKS)
    ]
    last = [
        flat + x_next * stack(mid[F:], out[F:]) + x_prev * stack(out[:F], mid[:F])
        for flat, mid, out in zip(in_plane(inner, coef[:5]), inner, outer)
    ]
    lane = lax.broadcasted_iota(jnp.int32, (2 * F, LANES), 1)
    slot = lane % NZ // 2
    packed = []
    for t in range(CHUNKS // 8):
        both = last[8 * t + 7]
        for g in range(7):
            both = jnp.where(slot == g, pltpu.roll(last[8 * t + g], LANES - 14 + 2 * g, 1), both)
        packed.append(both)
    sums = early_ref[SUMS : SUMS + 1, :]
    for p in range(2):
        for half in range(2):
            for z in range(MZ):
                j = half * MZ + z
                top = packed[2 * half + z % SIDES]
                row = (p * CHUNKS + j) * MESSAGE
                out_ref[row : row + F, :] = last[j][p * F : (p + 1) * F]
                out_ref[row + F : row + 2 * F, :] = top[p * F : (p + 1) * F]
                out_ref[row + 2 * F : row + MESSAGE, :] = sums


def halves(x):
    high = x.astype(jnp.bfloat16)
    return high, (x - high.astype(F32)).astype(jnp.bfloat16)


def gram_body(rows_ref, out_ref):
    first = lax.axis_index("mx") * MZ + lax.axis_index("side") * (MZ // SIDES)
    sums = rows_ref[pl.ds(first * MESSAGE + 2 * F, 8, stride=MESSAGE), :]
    lane = lax.broadcasted_iota(jnp.int32, (8, LANES), 1)
    chunk = lax.broadcasted_iota(jnp.int32, (8, LANES), 0)
    own_slot = lane % NZ // 2 == chunk
    moved = sums
    for g in range(1, 8):
        moved = jnp.where(chunk == g, pltpu.roll(sums, 2 * g, 1), moved)

    def spread(slot):
        tile = moved if slot == 0 else pltpu.roll(moved, LANES - 2 * slot, 1)
        return jnp.sum(jnp.where(own_slot, tile, 0.0), axis=0, keepdims=True)

    left, right = [], []
    for f in range(F):
        cells = rows_ref[pl.ds(F + f, MEMBERS, stride=MESSAGE), :]
        mean = jnp.sum(cells, axis=0, keepdims=True) * (1.0 / MEMBERS)
        deviation = cells - mean
        total = spread(f)
        drive = spread(F + f) - total * mean
        last = lax.broadcasted_iota(jnp.int32, (MEMBERS, LANES), 0) == MEMBERS - 1
        left.append(jnp.concatenate(halves(jnp.where(last, drive, deviation * total)), axis=0))
        right.append(jnp.concatenate(halves(deviation), axis=0))
    table = lax.dot_general(
        jnp.concatenate(left, axis=1),
        jnp.concatenate(right, axis=1),
        (((1,), (1,)), ((), ())),
        preferred_element_type=F32,
    )
    table = table[:MEMBERS] + table[MEMBERS:]
    table = table[:, :MEMBERS] + table[:, MEMBERS:]
    half = MEMBERS // 2
    upper, lower = table[:half], table[half:]
    lane = lax.broadcasted_iota(jnp.int32, (half, MEMBERS), 1)
    from_c = lax.broadcasted_iota(jnp.int32, (half, MEMBERS), 0) < lane
    swapped = jnp.concatenate([lower[:, half:], lower[:, :half]], axis=1)
    packed = jnp.where(jnp.logical_and(from_c, lane < half), swapped, upper)
    cross = jnp.concatenate([lower[half - 1 :]] * 2, axis=1)
    packed = jnp.concatenate([packed[: half // 2], packed[half // 2 :]], axis=1)
    out_ref[: TABLE - 1, :] = packed
    out_ref[TABLE - 1 :, :] = jnp.broadcast_to(cross, (out_ref.shape[0] - TABLE + 1, LANES))


def share_body(own_ref, other_ref, out_ref):
    table = own_ref[:TABLE] + other_ref[:TABLE]
    for i in range(out_ref.shape[0] // TABLE):
        out_ref[i * TABLE : (i + 1) * TABLE, :] = table


def mm(a, b):
    a_high, a_low = halves(a)
    b_high, b_low = halves(b)
    dot = functools.partial(jnp.dot, preferred_element_type=F32)
    return dot(a_high, b_high) + (dot(a_high, b_low) + dot(a_low, b_high))


def mix_body(table_ref, rows_ref, out_ref):
    rows = 8 * TABLE
    tables = table_ref[:rows]
    for i in range(1, table_ref.shape[0] // rows):
        tables = tables + table_ref[i * rows : (i + 1) * rows]
    table = tables[:TABLE]
    for i in range(1, 8):
        table = table + tables[i * TABLE : (i + 1) * TABLE]
    square = (MEMBERS, MEMBERS)
    half = MEMBERS // 2
    row = lax.broadcasted_iota(jnp.int32, square, 0)
    lane = lax.broadcasted_iota(jnp.int32, square, 1)
    identity = jnp.where(row == lane, 1.0, 0.0)
    upper = jnp.concatenate([table[: half // 2, :MEMBERS], table[: half // 2, MEMBERS:]], axis=0)
    swapped = jnp.concatenate([upper[:, half:], upper[:, :half]], axis=1)
    both = jnp.concatenate([upper, swapped], axis=0)
    keep = jnp.logical_or(
        jnp.logical_and(row < half, jnp.logical_or(lane >= half, row > lane)),
        jnp.logical_and(row >= half, row < lane),
    )
    off = jnp.where(keep, both, 0.0)
    off = off + jnp.transpose(off)
    diagonal = jnp.where(row < half, both, -jnp.sum(off, axis=1, keepdims=True))
    cross = jnp.sum(identity * table[TABLE - 1 :, :MEMBERS], axis=1, keepdims=True)
    system = jnp.where(row == lane, diagonal + (MEMBERS - 1.0), off)
    scale = jnp.sqrt(jnp.sum(system * system, keepdims=True))

    ensemble = jnp.concatenate(
        [rows_ref[pl.ds(f, MEMBERS, stride=MESSAGE), :] for f in range(F)], axis=1
    )
    centre = jnp.sum(ensemble, axis=0, keepdims=True) * (1.0 / MEMBERS)
    wide = jnp.concatenate(
        [ensemble - centre, jnp.broadcast_to(cross, (MEMBERS, LANES))], axis=1
    )

    root = system / scale
    inverse_root = 1.5 * identity - 0.5 * root
    root = mm(root, inverse_root)
    for step in range(1, NS_ITERS):
        factor = 1.5 * identity - 0.5 * mm(inverse_root, root)
        if step + 1 < NS_ITERS:
            both = mm(jnp.concatenate([root, inverse_root], axis=0), factor)
            root, inverse_root = both[:MEMBERS], both[MEMBERS:]
    wide = mm(factor, mm(inverse_root, wide))
    anomaly, drive = wide[:, : F * LANES], wide[:, F * LANES : F * LANES + 1] / scale
    shift = jnp.sum(drive * anomaly, axis=0, keepdims=True)
    mixed = (centre + shift) + anomaly * (math.sqrt(MEMBERS - 1.0) / jnp.sqrt(scale))
    for f in range(F):
        out_ref[pl.ds(f, MEMBERS, stride=F), :] = mixed[:, f * LANES : (f + 1) * LANES]


def exchange(rows, axes, peers):
    blocks = rows.reshape(peers, -1, 1, LANES)
    return lax.all_to_all(blocks, axes, split_axis=0, concat_axis=0, tiled=True)


def per_device(
    replica_profiles,
    diffusion,
    velocity,
    detector_voxel_position,
    detector_quantity_choice,
    sensor_value,
    sensor_var,
):
    slabs = lax.axis_size(SPACE)
    cells = replica_profiles.shape[2]
    own = replica_profiles.reshape(F, cells)
    pairs = [(i, i + 1) for i in range(0, slabs, 2)]
    beside = lax.ppermute(own, SPACE, pairs + [(b, a) for a, b in pairs])
    pairs = [(i, i + 1) for i in range(1, slabs - 1, 2)]
    across = lax.ppermute(own, SPACE, pairs + [(b, a) for a, b in pairs])
    early = call(
        early_body,
        (SUMS + 8, LANES),
        [SMEM, SMEM] + [VMEM] * 4,
        diffusion,
        velocity,
        detector_voxel_position.reshape(1, -1),
        detector_quantity_choice.reshape(1, -1),
        sensor_value.reshape(1, -1),
        sensor_var.reshape(1, -1),
        flops=FLOPS,
    )
    planes = call(own_body, (2 * FLAT, LANES), [VMEM] * 2, early, own, flops=FLOPS)
    fields = call(
        forecast_body,
        (MEMBERS * MESSAGE, LANES),
        [VMEM] * 4,
        early,
        planes,
        beside,
        across,
        flops=FLOPS,
    )
    rows = exchange(fields, MEMBER, MEMBERS).reshape(MEMBERS * MESSAGE, LANES)
    table = call(gram_body, (24, LANES), [VMEM], rows)
    other = lax.ppermute(table, "core", [(0, 1), (1, 0)])
    group = ("mx", "side", "y")
    peers = lax.axis_size(group)
    table = call(share_body, (peers * TABLE, LANES), [VMEM, VMEM], table, other)
    table = exchange(table, group, peers).reshape(peers * TABLE, LANES)
    mixed = call(mix_body, (MEMBERS * F, LANES), [VMEM, VMEM], table, rows)
    mixed = lax.all_to_all(
        mixed.reshape(MEMBERS, F, LANES), MEMBER, split_axis=0, concat_axis=0, tiled=True
    )
    return mixed.transpose(1, 0, 2).reshape(1, F, cells)


def solution(mesh):
    devices = mesh.devices.reshape(MX, MZ // SIDES, SIDES, -1, 2)
    fine = Mesh(devices, ("mx", "mz", "side", "y", "core"))
    sensors = P(MEMBER + SPACE)
    in_specs = (P(MEMBER, None, SPACE), P(), P(), sensors, sensors, sensors, sensors)
    return jax.shard_map(
        per_device,
        mesh=fine,
        in_specs=in_specs,
        out_specs=P(MEMBER, None, SPACE),
        check_vma=False,
    )
```

```python
import math

import jax
import jax.numpy as jnp
from jax import lax
from jax.experimental import pallas as pl
from jax.experimental.pallas import tpu as pltpu
from jax.sharding import Mesh, PartitionSpec as P

F = 4
NY = 256
NZ = 16
NS_ITERS = 5
MX = 4
MZ = 16
SIDES = 2
MEMBERS = MX * MZ
LANES = 128
PLANE = NY * NZ
CHUNKS = PLANE // LANES
FLAT = 8 * CHUNKS
SUMS = 8 * 7
FLOPS = 10**8
MESSAGE = 2 * F + 1
TABLE = MEMBERS * MEMBERS // 2 // LANES + 1

VMEM = pl.BlockSpec(memory_space=pltpu.VMEM)
SMEM = pl.BlockSpec(memory_space=pltpu.SMEM)
F32 = jnp.float32
MEMBER = ("mx", "mz", "side")
SPACE = ("y", "core")


def call(body, out_shape, in_specs, *operands, flops=None):
    return pl.pallas_call(
        body,
        out_shape=jax.ShapeDtypeStruct(out_shape, F32),
        in_specs=in_specs,
        out_specs=VMEM,
        cost_estimate=flops
        and pl.CostEstimate(flops=flops, bytes_accessed=1 << 18, transcendentals=0),
        compiler_params=pltpu.CompilerParams(vmem_limit_bytes=16 << 20),
    )(*operands)


def in_plane(centre, coef):
    keep, y_next, y_prev, z_next, z_prev = coef
    lane = lax.broadcasted_iota(jnp.int32, centre[0].shape, 1)
    up = [pltpu.roll(tile, LANES - NZ, 1) for tile in centre]
    down = [pltpu.roll(tile, NZ, 1) for tile in centre]
    zero = jnp.zeros_like(centre[0])
    result = []
    for j in range(CHUNKS):
        after = up[j + 1] if j + 1 < CHUNKS else zero
        before = down[j - 1] if j > 0 else zero
        result.append(
            keep * centre[j]
            + y_next * jnp.where(lane < LANES - NZ, up[j], after)
            + y_prev * jnp.where(lane >= NZ, down[j], before)
            + z_next * pltpu.roll(centre[j], LANES - 1, 1)
            + z_prev * pltpu.roll(centre[j], 1, 1)
        )
    return result


def stack(low, high):
    return jnp.concatenate([low, high], axis=0)


def sensor_sums(cell, choice, value, var):
    count = cell.shape[1]
    diagonal = lax.broadcasted_iota(jnp.int32, (count, count), 0) == lax.broadcasted_iota(
        jnp.int32, (count, count), 1
    )

    def column(row):
        return jnp.sum(jnp.where(diagonal, row, 0.0), axis=1, keepdims=True)

    weight = 1.0 / var
    spot = column((cell - 14 + 2 * choice).astype(F32)).astype(jnp.int32)
    lane = lax.broadcasted_iota(jnp.int32, (count, LANES), 1)
    share = jnp.where(spot == lane, column(weight), 0.0)
    share = share + jnp.where(spot + 2 * F == lane, column(weight * value), 0.0)
    return jnp.sum(share, axis=0, keepdims=True)


def early_body(diffusion_ref, velocity_ref, position_ref, choice_ref, value_ref, var_ref, out_ref):
    shape = (2 * F, LANES)
    field = lax.broadcasted_iota(jnp.int32, shape, 0) % F
    inner_z = lax.broadcasted_iota(jnp.int32, shape, 1) % NZ

    def per_field(values):
        tile = jnp.full(shape, values[F - 1], F32)
        for f in range(F - 1):
            tile = jnp.where(field == f, values[f], tile)
        return tile

    diffuse = per_field([diffusion_ref[f] for f in range(F)])
    move = [per_field([0.5 * velocity_ref[a, f] for f in range(F)]) for a in range(3)]
    coef = (
        1.0 - 6.0 * diffuse,
        diffuse - move[1],
        diffuse + move[1],
        jnp.where(inner_z != NZ - 1, diffuse - move[2], 0.0),
        jnp.where(inner_z != 0, diffuse + move[2], 0.0),
        diffuse - move[0],
        diffuse + move[0],
    )
    for i in range(len(coef)):
        out_ref[8 * i : 8 * i + 8, :] = coef[i]
    start = lax.axis_index(SPACE) * (2 * PLANE) + lax.axis_index(MEMBER) * LANES
    out_ref[SUMS : SUMS + 8, :] = jnp.broadcast_to(
        sensor_sums(position_ref[...] - start, choice_ref[...], value_ref[...], var_ref[...]), shape
    )


def own_body(early_ref, own_ref, out_ref):
    own = [stack(own_ref[:, tile(0, j)], own_ref[:, tile(1, j)]) for j in range(CHUNKS)]
    flat = in_plane(own, [early_ref[8 * i : 8 * i + 8, :] for i in range(5)])
    for j in range(CHUNKS):
        out_ref[8 * j : 8 * j + 8, :] = own[j]
        out_ref[FLAT + 8 * j : FLAT + 8 * j + 8, :] = flat[j]


def tile(plane, chunk):
    return slice(plane * PLANE + chunk * LANES, plane * PLANE + (chunk + 1) * LANES)


def forecast_body(early_ref, own_ref, beside_ref, across_ref, out_ref):
    slab = lax.axis_index(SPACE)
    even = slab % 2 == 0
    coef = [early_ref[8 * i : 8 * i + 8, :] for i in range(7)]
    x_next, x_prev = coef[5:]
    own = [own_ref[8 * j : 8 * j + 8, :] for j in range(CHUNKS)]

    def neighbour(first_ref, second_ref, plane, j):
        return jnp.where(even, first_ref[:, tile(plane, j)], second_ref[:, tile(plane, j)])

    left = [[neighbour(across_ref, beside_ref, p, j) for j in range(CHUNKS)] for p in range(2)]
    right = [[neighbour(beside_ref, across_ref, p, j) for j in range(CHUNKS)] for p in range(2)]
    upper = lax.broadcasted_iota(jnp.int32, (2 * F, LANES), 0) >= F
    inside = jnp.where(
        upper,
        jnp.where(slab < lax.axis_size(SPACE) - 1, 1.0, 0.0),
        jnp.where(slab > 0, 1.0, 0.0),
    )
    halo = [stack(left[1][j], right[0][j]) for j in range(CHUNKS)]
    halo_flat = in_plane(halo, coef[:5])
    outer = [
        inside
        * (
            halo_flat[j]
            + x_next * stack(own[j][:F], right[1][j])
            + x_prev * stack(left[0][j], own[j][F:])
        )
        for j in range(CHUNKS)
    ]
    inner = [
        own_ref[FLAT + 8 * j : FLAT + 8 * j + 8, :]
        + x_next * stack(own[j][F:], halo[j][F:])
        + x_prev * stack(halo[j][:F], own[j][:F])
        for j in range(CHUNKS)
    ]
    last = [
        flat + x_next * stack(mid[F:], out[F:]) + x_prev * stack(out[:F], mid[:F])
        for flat, mid, out in zip(in_plane(inner, coef[:5]), inner, outer)
    ]
    lane = lax.broadcasted_iota(jnp.int32, (2 * F, LANES), 1)
    slot = lane % NZ // 2
    packed = []
    for t in range(CHUNKS // 8):
        both = last[8 * t + 7]
        for g in range(7):
            both = jnp.where(slot == g, pltpu.roll(last[8 * t + g], LANES - 14 + 2 * g, 1), both)
        packed.append(both)
    sums = early_ref[SUMS : SUMS + 1, :]
    for p in range(2):
        for half in range(2):
            for z in range(MZ):
                j = half * MZ + z
                top = packed[2 * half + z % SIDES]
                row = (p * CHUNKS + j) * MESSAGE
                out_ref[row : row + F, :] = last[j][p * F : (p + 1) * F]
                out_ref[row + F : row + 2 * F, :] = top[p * F : (p + 1) * F]
                out_ref[row + 2 * F : row + MESSAGE, :] = sums


def halves(x):
    high = x.astype(jnp.bfloat16)
    return high, (x - high.astype(F32)).astype(jnp.bfloat16)


def gram_body(rows_ref, out_ref):
    first = lax.axis_index("mx") * MZ + lax.axis_index("side") * (MZ // SIDES)
    sums = rows_ref[pl.ds(first * MESSAGE + 2 * F, 8, stride=MESSAGE), :]
    lane = lax.broadcasted_iota(jnp.int32, (8, LANES), 1)
    chunk = lax.broadcasted_iota(jnp.int32, (8, LANES), 0)
    own_slot = lane % NZ // 2 == chunk
    moved = sums
    for g in range(1, 8):
        moved = jnp.where(chunk == g, pltpu.roll(sums, 2 * g, 1), moved)

    def spread(slot):
        tile = moved if slot == 0 else pltpu.roll(moved, LANES - 2 * slot, 1)
        return jnp.sum(jnp.where(own_slot, tile, 0.0), axis=0, keepdims=True)

    left, right = [], []
    for f in range(F):
        cells = rows_ref[pl.ds(F + f, MEMBERS, stride=MESSAGE), :]
        mean = jnp.sum(cells, axis=0, keepdims=True) * (1.0 / MEMBERS)
        deviation = cells - mean
        total = spread(f)
        drive = spread(F + f) - total * mean
        last = lax.broadcasted_iota(jnp.int32, (MEMBERS, LANES), 0) == MEMBERS - 1
        left.append(jnp.concatenate(halves(jnp.where(last, drive, deviation * total)), axis=0))
        right.append(jnp.concatenate(halves(deviation), axis=0))
    table = lax.dot_general(
        jnp.concatenate(left, axis=1),
        jnp.concatenate(right, axis=1),
        (((1,), (1,)), ((), ())),
        preferred_element_type=F32,
    )
    table = table[:MEMBERS] + table[MEMBERS:]
    table = table[:, :MEMBERS] + table[:, MEMBERS:]
    half = MEMBERS // 2
    upper, lower = table[:half], table[half:]
    lane = lax.broadcasted_iota(jnp.int32, (half, MEMBERS), 1)
    from_c = lax.broadcasted_iota(jnp.int32, (half, MEMBERS), 0) < lane
    swapped = jnp.concatenate([lower[:, half:], lower[:, :half]], axis=1)
    packed = jnp.where(jnp.logical_and(from_c, lane < half), swapped, upper)
    cross = jnp.concatenate([lower[half - 1 :]] * 2, axis=1)
    packed = jnp.concatenate([packed[: half // 2], packed[half // 2 :]], axis=1)
    out_ref[: TABLE - 1, :] = packed
    out_ref[TABLE - 1 :, :] = jnp.broadcast_to(cross, (out_ref.shape[0] - TABLE + 1, LANES))


def share_body(own_ref, other_ref, out_ref):
    table = own_ref[:TABLE] + other_ref[:TABLE]
    for i in range(out_ref.shape[0] // TABLE):
        out_ref[i * TABLE : (i + 1) * TABLE, :] = table


def mm(a, b):
    product = jnp.dot(
        jnp.concatenate(halves(a), axis=0),
        jnp.concatenate(halves(b), axis=0),
        preferred_element_type=F32,
    )
    rows = a.shape[0]
    return product[:rows] + product[rows:]


def mix_body(table_ref, rows_ref, out_ref):
    rows = 8 * TABLE
    tables = table_ref[:rows]
    for i in range(1, table_ref.shape[0] // rows):
        tables = tables + table_ref[i * rows : (i + 1) * rows]
    table = tables[:TABLE]
    for i in range(1, 8):
        table = table + tables[i * TABLE : (i + 1) * TABLE]
    square = (MEMBERS, MEMBERS)
    half = MEMBERS // 2
    row = lax.broadcasted_iota(jnp.int32, square, 0)
    lane = lax.broadcasted_iota(jnp.int32, square, 1)
    identity = jnp.where(row == lane, 1.0, 0.0)
    upper = jnp.concatenate([table[: half // 2, :MEMBERS], table[: half // 2, MEMBERS:]], axis=0)
    swapped = jnp.concatenate([upper[:, half:], upper[:, :half]], axis=1)
    both = jnp.concatenate([upper, swapped], axis=0)
    keep = jnp.logical_or(
        jnp.logical_and(row < half, jnp.logical_or(lane >= half, row > lane)),
        jnp.logical_and(row >= half, row < lane),
    )
    off = jnp.where(keep, both, 0.0)
    off = off + jnp.transpose(off)
    diagonal = jnp.where(row < half, both, -jnp.sum(off, axis=1, keepdims=True))
    cross = jnp.sum(identity * table[TABLE - 1 :, :MEMBERS], axis=1, keepdims=True)
    system = jnp.where(row == lane, diagonal + (MEMBERS - 1.0), off)
    scale = jnp.sqrt(jnp.sum(system * system, keepdims=True))
    identity, system = (jnp.concatenate([x, x], axis=1) for x in (identity, system))

    ensemble = jnp.concatenate(
        [rows_ref[pl.ds(f, MEMBERS, stride=MESSAGE), :] for f in range(F)], axis=1
    )
    centre = jnp.sum(ensemble, axis=0, keepdims=True) * (1.0 / MEMBERS)
    wide = jnp.concatenate(
        [ensemble - centre, jnp.broadcast_to(cross, (MEMBERS, LANES))], axis=1
    )

    root = system / scale
    inverse_root = 1.5 * identity - 0.5 * root
    root = mm(root, inverse_root)
    for step in range(1, NS_ITERS):
        factor = 1.5 * identity - 0.5 * mm(inverse_root, root)
        if step + 1 < NS_ITERS:
            both = mm(jnp.concatenate([root, inverse_root], axis=0), factor)
            root, inverse_root = both[:MEMBERS], both[MEMBERS:]
    wide = mm(factor, mm(inverse_root, wide))
    anomaly, drive = wide[:, : F * LANES], wide[:, F * LANES : F * LANES + 1] / scale
    shift = jnp.sum(drive * anomaly, axis=0, keepdims=True)
    mixed = (centre + shift) + anomaly * (math.sqrt(MEMBERS - 1.0) / jnp.sqrt(scale))
    for f in range(F):
        out_ref[pl.ds(f, MEMBERS, stride=F), :] = mixed[:, f * LANES : (f + 1) * LANES]


def exchange(rows, axes, peers):
    blocks = rows.reshape(peers, -1, 1, LANES)
    return lax.all_to_all(blocks, axes, split_axis=0, concat_axis=0, tiled=True)


def per_device(
    replica_profiles,
    diffusion,
    velocity,
    detector_voxel_position,
    detector_quantity_choice,
    sensor_value,
    sensor_var,
):
    slabs = lax.axis_size(SPACE)
    cells = replica_profiles.shape[2]
    own = replica_profiles.reshape(F, cells)
    pairs = [(i, i + 1) for i in range(0, slabs, 2)]
    beside = lax.ppermute(own, SPACE, pairs + [(b, a) for a, b in pairs])
    pairs = [(i, i + 1) for i in range(1, slabs - 1, 2)]
    across = lax.ppermute(own, SPACE, pairs + [(b, a) for a, b in pairs])
    early = call(
        early_body,
        (SUMS + 8, LANES),
        [SMEM, SMEM] + [VMEM] * 4,
        diffusion,
        velocity,
        detector_voxel_position.reshape(1, -1),
        detector_quantity_choice.reshape(1, -1),
        sensor_value.reshape(1, -1),
        sensor_var.reshape(1, -1),
        flops=FLOPS,
    )
    planes = call(own_body, (2 * FLAT, LANES), [VMEM] * 2, early, own, flops=FLOPS)
    fields = call(
        forecast_body,
        (MEMBERS * MESSAGE, LANES),
        [VMEM] * 4,
        early,
        planes,
        beside,
        across,
        flops=FLOPS,
    )
    rows = exchange(fields, MEMBER, MEMBERS).reshape(MEMBERS * MESSAGE, LANES)
    table = call(gram_body, (24, LANES), [VMEM], rows)
    other = lax.ppermute(table, "core", [(0, 1), (1, 0)])
    group = ("mx", "side", "y")
    peers = lax.axis_size(group)
    table = call(share_body, (peers * TABLE, LANES), [VMEM, VMEM], table, other)
    table = exchange(table, group, peers).reshape(peers * TABLE, LANES)
    mixed = call(mix_body, (MEMBERS * F, LANES), [VMEM, VMEM], table, rows)
    mixed = lax.all_to_all(
        mixed.reshape(MEMBERS, F, LANES), MEMBER, split_axis=0, concat_axis=0, tiled=True
    )
    return mixed.transpose(1, 0, 2).reshape(1, F, cells)


def solution(mesh):
    devices = mesh.devices.reshape(MX, MZ // SIDES, SIDES, -1, 2)
    fine = Mesh(devices, ("mx", "mz", "side", "y", "core"))
    sensors = P(MEMBER + SPACE)
    in_specs = (P(MEMBER, None, SPACE), P(), P(), sensors, sensors, sensors, sensors)
    return jax.shard_map(
        per_device,
        mesh=fine,
        in_specs=in_specs,
        out_specs=P(MEMBER, None, SPACE),
        check_vma=False,
    )
```

```python
import math

import jax
import jax.numpy as jnp
from jax import lax
from jax.experimental import pallas as pl
from jax.experimental.pallas import tpu as pltpu
from jax.sharding import Mesh, PartitionSpec as P

F = 4
NY = 256
NZ = 16
NS_ITERS = 5
MX = 4
MZ = 16
SIDES = 2
MEMBERS = MX * MZ
LANES = 128
PLANE = NY * NZ
CHUNKS = PLANE // LANES
FLAT = 8 * CHUNKS
SUMS = 8 * 7
FLOPS = 10**8
MESSAGE = 2 * F + 1
TABLE = MEMBERS * MEMBERS // 2 // LANES + 1

VMEM = pl.BlockSpec(memory_space=pltpu.VMEM)
SMEM = pl.BlockSpec(memory_space=pltpu.SMEM)
F32 = jnp.float32
MEMBER = ("mx", "mz", "side")
SPACE = ("y", "core")


def call(body, out_shape, in_specs, *operands, flops=None):
    return pl.pallas_call(
        body,
        out_shape=jax.ShapeDtypeStruct(out_shape, F32),
        in_specs=in_specs,
        out_specs=VMEM,
        cost_estimate=flops
        and pl.CostEstimate(flops=flops, bytes_accessed=1 << 18, transcendentals=0),
        compiler_params=pltpu.CompilerParams(vmem_limit_bytes=16 << 20),
    )(*operands)


def in_plane(centre, coef):
    keep, y_next, y_prev, z_next, z_prev = coef
    lane = lax.broadcasted_iota(jnp.int32, centre[0].shape, 1)
    up = [pltpu.roll(tile, LANES - NZ, 1) for tile in centre]
    down = [pltpu.roll(tile, NZ, 1) for tile in centre]
    zero = jnp.zeros_like(centre[0])
    result = []
    for j in range(CHUNKS):
        after = up[j + 1] if j + 1 < CHUNKS else zero
        before = down[j - 1] if j > 0 else zero
        result.append(
            keep * centre[j]
            + y_next * jnp.where(lane < LANES - NZ, up[j], after)
            + y_prev * jnp.where(lane >= NZ, down[j], before)
            + z_next * pltpu.roll(centre[j], LANES - 1, 1)
            + z_prev * pltpu.roll(centre[j], 1, 1)
        )
    return result


def stack(low, high):
    return jnp.concatenate([low, high], axis=0)


def sensor_sums(cell, choice, value, var):
    count = cell.shape[1]
    diagonal = lax.broadcasted_iota(jnp.int32, (count, count), 0) == lax.broadcasted_iota(
        jnp.int32, (count, count), 1
    )

    def column(row):
        return jnp.sum(jnp.where(diagonal, row, 0.0), axis=1, keepdims=True)

    weight = 1.0 / var
    spot = column((cell - 14 + 2 * choice).astype(F32)).astype(jnp.int32)
    lane = lax.broadcasted_iota(jnp.int32, (count, LANES), 1)
    share = jnp.where(spot == lane, column(weight), 0.0)
    share = share + jnp.where(spot + 2 * F == lane, column(weight * value), 0.0)
    return jnp.sum(share, axis=0, keepdims=True)


def early_body(diffusion_ref, velocity_ref, position_ref, choice_ref, value_ref, var_ref, out_ref):
    shape = (2 * F, LANES)
    field = lax.broadcasted_iota(jnp.int32, shape, 0) % F
    inner_z = lax.broadcasted_iota(jnp.int32, shape, 1) % NZ

    def per_field(values):
        tile = jnp.full(shape, values[F - 1], F32)
        for f in range(F - 1):
            tile = jnp.where(field == f, values[f], tile)
        return tile

    diffuse = per_field([diffusion_ref[f] for f in range(F)])
    move = [per_field([0.5 * velocity_ref[a, f] for f in range(F)]) for a in range(3)]
    coef = (
        1.0 - 6.0 * diffuse,
        diffuse - move[1],
        diffuse + move[1],
        jnp.where(inner_z != NZ - 1, diffuse - move[2], 0.0),
        jnp.where(inner_z != 0, diffuse + move[2], 0.0),
        diffuse - move[0],
        diffuse + move[0],
    )
    for i in range(len(coef)):
        out_ref[8 * i : 8 * i + 8, :] = coef[i]
    start = lax.axis_index(SPACE) * (2 * PLANE) + lax.axis_index(MEMBER) * LANES
    out_ref[SUMS : SUMS + 8, :] = jnp.broadcast_to(
        sensor_sums(position_ref[...] - start, choice_ref[...], value_ref[...], var_ref[...]), shape
    )


def own_body(early_ref, own_ref, out_ref):
    own = [stack(own_ref[:, tile(0, j)], own_ref[:, tile(1, j)]) for j in range(CHUNKS)]
    flat = in_plane(own, [early_ref[8 * i : 8 * i + 8, :] for i in range(5)])
    for j in range(CHUNKS):
        out_ref[8 * j : 8 * j + 8, :] = own[j]
        out_ref[FLAT + 8 * j : FLAT + 8 * j + 8, :] = flat[j]


def tile(plane, chunk):
    return slice(plane * PLANE + chunk * LANES, plane * PLANE + (chunk + 1) * LANES)


def forecast_body(early_ref, own_ref, beside_ref, across_ref, out_ref):
    slab = lax.axis_index(SPACE)
    even = slab % 2 == 0
    coef = [early_ref[8 * i : 8 * i + 8, :] for i in range(7)]
    x_next, x_prev = coef[5:]
    own = [own_ref[8 * j : 8 * j + 8, :] for j in range(CHUNKS)]

    def neighbour(first_ref, second_ref, plane, j):
        return jnp.where(even, first_ref[:, tile(plane, j)], second_ref[:, tile(plane, j)])

    left = [[neighbour(across_ref, beside_ref, p, j) for j in range(CHUNKS)] for p in range(2)]
    right = [[neighbour(beside_ref, across_ref, p, j) for j in range(CHUNKS)] for p in range(2)]
    upper = lax.broadcasted_iota(jnp.int32, (2 * F, LANES), 0) >= F
    inside = jnp.where(
        upper,
        jnp.where(slab < lax.axis_size(SPACE) - 1, 1.0, 0.0),
        jnp.where(slab > 0, 1.0, 0.0),
    )
    halo = [stack(left[1][j], right[0][j]) for j in range(CHUNKS)]
    halo_flat = in_plane(halo, coef[:5])
    outer = [
        inside
        * (
            halo_flat[j]
            + x_next * stack(own[j][:F], right[1][j])
            + x_prev * stack(left[0][j], own[j][F:])
        )
        for j in range(CHUNKS)
    ]
    inner = [
        own_ref[FLAT + 8 * j : FLAT + 8 * j + 8, :]
        + x_next * stack(own[j][F:], halo[j][F:])
        + x_prev * stack(halo[j][:F], own[j][:F])
        for j in range(CHUNKS)
    ]
    last = [
        flat + x_next * stack(mid[F:], out[F:]) + x_prev * stack(out[:F], mid[:F])
        for flat, mid, out in zip(in_plane(inner, coef[:5]), inner, outer)
    ]
    lane = lax.broadcasted_iota(jnp.int32, (2 * F, LANES), 1)
    slot = lane % NZ // 2
    packed = []
    for t in range(CHUNKS // 8):
        both = last[8 * t + 7]
        for g in range(7):
            both = jnp.where(slot == g, pltpu.roll(last[8 * t + g], LANES - 14 + 2 * g, 1), both)
        packed.append(both)
    sums = early_ref[SUMS : SUMS + 1, :]
    for p in range(2):
        for half in range(2):
            for z in range(MZ):
                j = half * MZ + z
                top = packed[2 * half + z % SIDES]
                row = (p * CHUNKS + j) * MESSAGE
                out_ref[row : row + F, :] = last[j][p * F : (p + 1) * F]
                out_ref[row + F : row + 2 * F, :] = top[p * F : (p + 1) * F]
                out_ref[row + 2 * F : row + MESSAGE, :] = sums


def halves(x):
    high = x.astype(jnp.bfloat16)
    return high, (x - high.astype(F32)).astype(jnp.bfloat16)


def gram_body(rows_ref, out_ref):
    first = lax.axis_index("mx") * MZ + lax.axis_index("side") * (MZ // SIDES)
    sums = rows_ref[pl.ds(first * MESSAGE + 2 * F, 8, stride=MESSAGE), :]
    lane = lax.broadcasted_iota(jnp.int32, (8, LANES), 1)
    chunk = lax.broadcasted_iota(jnp.int32, (8, LANES), 0)
    own_slot = lane % NZ // 2 == chunk
    moved = sums
    for g in range(1, 8):
        moved = jnp.where(chunk == g, pltpu.roll(sums, 2 * g, 1), moved)

    def spread(slot):
        tile = moved if slot == 0 else pltpu.roll(moved, LANES - 2 * slot, 1)
        return jnp.sum(jnp.where(own_slot, tile, 0.0), axis=0, keepdims=True)

    left, right = [], []
    for f in range(F):
        cells = rows_ref[pl.ds(F + f, MEMBERS, stride=MESSAGE), :]
        mean = jnp.sum(cells, axis=0, keepdims=True) * (1.0 / MEMBERS)
        deviation = cells - mean
        total = spread(f)
        drive = spread(F + f) - total * mean
        last = lax.broadcasted_iota(jnp.int32, (MEMBERS, LANES), 0) == MEMBERS - 1
        left.append(jnp.concatenate(halves(jnp.where(last, drive, deviation * total)), axis=0))
        right.append(jnp.concatenate(halves(deviation), axis=0))
    table = lax.dot_general(
        jnp.concatenate(left, axis=1),
        jnp.concatenate(right, axis=1),
        (((1,), (1,)), ((), ())),
        preferred_element_type=F32,
    )
    table = table[:MEMBERS] + table[MEMBERS:]
    table = table[:, :MEMBERS] + table[:, MEMBERS:]
    half = MEMBERS // 2
    upper, lower = table[:half], table[half:]
    lane = lax.broadcasted_iota(jnp.int32, (half, MEMBERS), 1)
    from_c = lax.broadcasted_iota(jnp.int32, (half, MEMBERS), 0) < lane
    swapped = jnp.concatenate([lower[:, half:], lower[:, :half]], axis=1)
    packed = jnp.where(jnp.logical_and(from_c, lane < half), swapped, upper)
    cross = jnp.concatenate([lower[half - 1 :]] * 2, axis=1)
    packed = jnp.concatenate([packed[: half // 2], packed[half // 2 :]], axis=1)
    for i in range(out_ref.shape[0] // TABLE):
        out_ref[i * TABLE : (i + 1) * TABLE - 1, :] = packed
        out_ref[(i + 1) * TABLE - 1 : (i + 1) * TABLE, :] = cross


def table_sum(table_ref):
    rows = 8 * TABLE
    tables = table_ref[:rows]
    for i in range(1, table_ref.shape[0] // rows):
        tables = tables + table_ref[i * rows : (i + 1) * rows]
    table = tables[:TABLE]
    for i in range(1, 8):
        table = table + tables[i * TABLE : (i + 1) * TABLE]
    return table


def share_body(table_ref, out_ref):
    table = table_sum(table_ref)
    for i in range(out_ref.shape[0] // TABLE):
        out_ref[i * TABLE : (i + 1) * TABLE, :] = table


def mm(a, b):
    product = jnp.dot(
        jnp.concatenate(halves(a), axis=0),
        jnp.concatenate(halves(b), axis=0),
        preferred_element_type=F32,
    )
    rows = a.shape[0]
    return product[:rows] + product[rows:]


def mix_body(table_ref, rows_ref, out_ref):
    table = table_sum(table_ref)
    square = (MEMBERS, MEMBERS)
    half = MEMBERS // 2
    row = lax.broadcasted_iota(jnp.int32, square, 0)
    lane = lax.broadcasted_iota(jnp.int32, square, 1)
    identity = jnp.where(row == lane, 1.0, 0.0)
    upper = jnp.concatenate([table[: half // 2, :MEMBERS], table[: half // 2, MEMBERS:]], axis=0)
    swapped = jnp.concatenate([upper[:, half:], upper[:, :half]], axis=1)
    both = jnp.concatenate([upper, swapped], axis=0)
    keep = jnp.logical_or(
        jnp.logical_and(row < half, jnp.logical_or(lane >= half, row > lane)),
        jnp.logical_and(row >= half, row < lane),
    )
    off = jnp.where(keep, both, 0.0)
    off = off + jnp.transpose(off)
    diagonal = jnp.where(row < half, both, -jnp.sum(off, axis=1, keepdims=True))
    cross = jnp.sum(identity * table[TABLE - 1 :, :MEMBERS], axis=1, keepdims=True)
    system = jnp.where(row == lane, diagonal + (MEMBERS - 1.0), off)
    scale = jnp.sqrt(jnp.sum(system * system, keepdims=True))
    identity, system = (jnp.concatenate([x, x], axis=1) for x in (identity, system))

    ensemble = jnp.concatenate(
        [rows_ref[pl.ds(f, MEMBERS, stride=MESSAGE), :] for f in range(F)], axis=1
    )
    centre = jnp.sum(ensemble, axis=0, keepdims=True) * (1.0 / MEMBERS)
    wide = jnp.concatenate(
        [ensemble - centre, jnp.broadcast_to(cross, (MEMBERS, LANES))], axis=1
    )

    root = system / scale
    inverse_root = 1.5 * identity - 0.5 * root
    root = mm(root, inverse_root)
    for step in range(1, NS_ITERS):
        factor = 1.5 * identity - 0.5 * mm(inverse_root, root)
        if step + 1 < NS_ITERS:
            both = mm(jnp.concatenate([root, inverse_root], axis=0), factor)
            root, inverse_root = both[:MEMBERS], both[MEMBERS:]
    wide = mm(factor, mm(inverse_root, wide))
    anomaly, drive = wide[:, : F * LANES], wide[:, F * LANES : F * LANES + 1] / scale
    shift = jnp.sum(drive * anomaly, axis=0, keepdims=True)
    mixed = (centre + shift) + anomaly * (math.sqrt(MEMBERS - 1.0) / jnp.sqrt(scale))
    for f in range(F):
        out_ref[pl.ds(f, MEMBERS, stride=F), :] = mixed[:, f * LANES : (f + 1) * LANES]


def exchange(rows, axes, peers):
    blocks = rows.reshape(peers, -1, 1, LANES)
    return lax.all_to_all(blocks, axes, split_axis=0, concat_axis=0, tiled=True)


def per_device(
    replica_profiles,
    diffusion,
    velocity,
    detector_voxel_position,
    detector_quantity_choice,
    sensor_value,
    sensor_var,
):
    slabs = lax.axis_size(SPACE)
    cells = replica_profiles.shape[2]
    own = replica_profiles.reshape(F, cells)
    pairs = [(i, i + 1) for i in range(0, slabs, 2)]
    beside = lax.ppermute(own, SPACE, pairs + [(b, a) for a, b in pairs])
    pairs = [(i, i + 1) for i in range(1, slabs - 1, 2)]
    across = lax.ppermute(own, SPACE, pairs + [(b, a) for a, b in pairs])
    early = call(
        early_body,
        (SUMS + 8, LANES),
        [SMEM, SMEM] + [VMEM] * 4,
        diffusion,
        velocity,
        detector_voxel_position.reshape(1, -1),
        detector_quantity_choice.reshape(1, -1),
        sensor_value.reshape(1, -1),
        sensor_var.reshape(1, -1),
        flops=FLOPS,
    )
    planes = call(own_body, (2 * FLAT, LANES), [VMEM] * 2, early, own, flops=FLOPS)
    fields = call(
        forecast_body,
        (MEMBERS * MESSAGE, LANES),
        [VMEM] * 4,
        early,
        planes,
        beside,
        across,
        flops=FLOPS,
    )
    rows = exchange(fields, MEMBER, MEMBERS).reshape(MEMBERS * MESSAGE, LANES)
    table = call(gram_body, (slabs * TABLE, LANES), [VMEM], rows)
    table = exchange(table, SPACE, slabs).reshape(slabs * TABLE, LANES)
    group = ("mx", "side")
    peers = lax.axis_size(group)
    table = call(share_body, (peers * TABLE, LANES), [VMEM], table)
    table = exchange(table, group, peers).reshape(peers * TABLE, LANES)
    mixed = call(mix_body, (MEMBERS * F, LANES), [VMEM, VMEM], table, rows)
    mixed = lax.all_to_all(
        mixed.reshape(MEMBERS, F, LANES), MEMBER, split_axis=0, concat_axis=0, tiled=True
    )
    return mixed.transpose(1, 0, 2).reshape(1, F, cells)


def solution(mesh):
    devices = mesh.devices.reshape(MX, MZ // SIDES, SIDES, -1, 2)
    fine = Mesh(devices, ("mx", "mz", "side", "y", "core"))
    sensors = P(MEMBER + SPACE)
    in_specs = (P(MEMBER, None, SPACE), P(), P(), sensors, sensors, sensors, sensors)
    return jax.shard_map(
        per_device,
        mesh=fine,
        in_specs=in_specs,
        out_specs=P(MEMBER, None, SPACE),
        check_vma=False,
    )
```

```python
import math

import jax
import jax.numpy as jnp
from jax import lax
from jax.experimental import pallas as pl
from jax.experimental.pallas import tpu as pltpu
from jax.sharding import Mesh, PartitionSpec as P

F = 4
NY = 256
NZ = 16
NS_ITERS = 5
MX = 4
MZ = 16
SIDES = 2
MEMBERS = MX * MZ
LANES = 128
PLANE = NY * NZ
CHUNKS = PLANE // LANES
FLAT = 8 * CHUNKS
SUMS = 8 * 7
FLOPS = 10**8
MESSAGE = 2 * F + 1
TABLE = MEMBERS * MEMBERS // 2 // LANES + 1

VMEM = pl.BlockSpec(memory_space=pltpu.VMEM)
SMEM = pl.BlockSpec(memory_space=pltpu.SMEM)
F32 = jnp.float32
MEMBER = ("mx", "mz", "side")
SPACE = ("y", "core")


def call(body, out_shape, in_specs, *operands, flops=None):
    return pl.pallas_call(
        body,
        out_shape=jax.ShapeDtypeStruct(out_shape, F32),
        in_specs=in_specs,
        out_specs=VMEM,
        cost_estimate=flops
        and pl.CostEstimate(flops=flops, bytes_accessed=1 << 18, transcendentals=0),
        compiler_params=pltpu.CompilerParams(vmem_limit_bytes=16 << 20),
    )(*operands)


def in_plane(centre, coef):
    keep, y_next, y_prev, z_next, z_prev = coef
    lane = lax.broadcasted_iota(jnp.int32, centre[0].shape, 1)
    up = [pltpu.roll(tile, LANES - NZ, 1) for tile in centre]
    down = [pltpu.roll(tile, NZ, 1) for tile in centre]
    zero = jnp.zeros_like(centre[0])
    result = []
    for j in range(CHUNKS):
        after = up[j + 1] if j + 1 < CHUNKS else zero
        before = down[j - 1] if j > 0 else zero
        result.append(
            keep * centre[j]
            + y_next * jnp.where(lane < LANES - NZ, up[j], after)
            + y_prev * jnp.where(lane >= NZ, down[j], before)
            + z_next * pltpu.roll(centre[j], LANES - 1, 1)
            + z_prev * pltpu.roll(centre[j], 1, 1)
        )
    return result


def stack(low, high):
    return jnp.concatenate([low, high], axis=0)


def sensor_sums(cell, choice, value, var):
    count = cell.shape[1]
    diagonal = lax.broadcasted_iota(jnp.int32, (count, count), 0) == lax.broadcasted_iota(
        jnp.int32, (count, count), 1
    )

    def column(row):
        return jnp.sum(jnp.where(diagonal, row, 0.0), axis=1, keepdims=True)

    weight = 1.0 / var
    spot = column((cell - 14 + 2 * choice).astype(F32)).astype(jnp.int32)
    lane = lax.broadcasted_iota(jnp.int32, (count, LANES), 1)
    share = jnp.where(spot == lane, column(weight), 0.0)
    share = share + jnp.where(spot + 2 * F == lane, column(weight * value), 0.0)
    return jnp.sum(share, axis=0, keepdims=True)


def early_body(diffusion_ref, velocity_ref, position_ref, choice_ref, value_ref, var_ref, out_ref):
    shape = (2 * F, LANES)
    field = lax.broadcasted_iota(jnp.int32, shape, 0) % F
    inner_z = lax.broadcasted_iota(jnp.int32, shape, 1) % NZ

    def per_field(values):
        tile = jnp.full(shape, values[F - 1], F32)
        for f in range(F - 1):
            tile = jnp.where(field == f, values[f], tile)
        return tile

    diffuse = per_field([diffusion_ref[f] for f in range(F)])
    move = [per_field([0.5 * velocity_ref[a, f] for f in range(F)]) for a in range(3)]
    coef = (
        1.0 - 6.0 * diffuse,
        diffuse - move[1],
        diffuse + move[1],
        jnp.where(inner_z != NZ - 1, diffuse - move[2], 0.0),
        jnp.where(inner_z != 0, diffuse + move[2], 0.0),
        diffuse - move[0],
        diffuse + move[0],
    )
    for i in range(len(coef)):
        out_ref[8 * i : 8 * i + 8, :] = coef[i]
    start = lax.axis_index(SPACE) * (2 * PLANE) + lax.axis_index(MEMBER) * LANES
    out_ref[SUMS : SUMS + 8, :] = jnp.broadcast_to(
        sensor_sums(position_ref[...] - start, choice_ref[...], value_ref[...], var_ref[...]), shape
    )


def own_body(early_ref, own_ref, out_ref):
    own = [stack(own_ref[:, tile(0, j)], own_ref[:, tile(1, j)]) for j in range(CHUNKS)]
    flat = in_plane(own, [early_ref[8 * i : 8 * i + 8, :] for i in range(5)])
    for j in range(CHUNKS):
        out_ref[8 * j : 8 * j + 8, :] = own[j]
        out_ref[FLAT + 8 * j : FLAT + 8 * j + 8, :] = flat[j]


def tile(plane, chunk):
    return slice(plane * PLANE + chunk * LANES, plane * PLANE + (chunk + 1) * LANES)


def forecast_body(early_ref, own_ref, beside_ref, across_ref, out_ref):
    slab = lax.axis_index(SPACE)
    even = slab % 2 == 0
    coef = [early_ref[8 * i : 8 * i + 8, :] for i in range(7)]
    x_next, x_prev = coef[5:]
    own = [own_ref[8 * j : 8 * j + 8, :] for j in range(CHUNKS)]

    def neighbour(first_ref, second_ref, plane, j):
        return jnp.where(even, first_ref[:, tile(plane, j)], second_ref[:, tile(plane, j)])

    left = [[neighbour(across_ref, beside_ref, p, j) for j in range(CHUNKS)] for p in range(2)]
    right = [[neighbour(beside_ref, across_ref, p, j) for j in range(CHUNKS)] for p in range(2)]
    upper = lax.broadcasted_iota(jnp.int32, (2 * F, LANES), 0) >= F
    inside = jnp.where(
        upper,
        jnp.where(slab < lax.axis_size(SPACE) - 1, 1.0, 0.0),
        jnp.where(slab > 0, 1.0, 0.0),
    )
    halo = [stack(left[1][j], right[0][j]) for j in range(CHUNKS)]
    halo_flat = in_plane(halo, coef[:5])
    outer = [
        inside
        * (
            halo_flat[j]
            + x_next * stack(own[j][:F], right[1][j])
            + x_prev * stack(left[0][j], own[j][F:])
        )
        for j in range(CHUNKS)
    ]
    inner = [
        own_ref[FLAT + 8 * j : FLAT + 8 * j + 8, :]
        + x_next * stack(own[j][F:], halo[j][F:])
        + x_prev * stack(halo[j][:F], own[j][:F])
        for j in range(CHUNKS)
    ]
    last = [
        flat + x_next * stack(mid[F:], out[F:]) + x_prev * stack(out[:F], mid[:F])
        for flat, mid, out in zip(in_plane(inner, coef[:5]), inner, outer)
    ]
    lane = lax.broadcasted_iota(jnp.int32, (2 * F, LANES), 1)
    slot = lane % NZ // 2
    packed = []
    for t in range(CHUNKS // 8):
        both = last[8 * t + 7]
        for g in range(7):
            both = jnp.where(slot == g, pltpu.roll(last[8 * t + g], LANES - 14 + 2 * g, 1), both)
        packed.append(both)
    sums = early_ref[SUMS : SUMS + 1, :]
    for p in range(2):
        for half in range(2):
            for z in range(MZ):
                j = half * MZ + z
                top = packed[2 * half + z % SIDES]
                row = (p * CHUNKS + j) * MESSAGE
                out_ref[row : row + F, :] = last[j][p * F : (p + 1) * F]
                out_ref[row + F : row + 2 * F, :] = top[p * F : (p + 1) * F]
                out_ref[row + 2 * F : row + MESSAGE, :] = sums


def halves(x):
    high = x.astype(jnp.bfloat16)
    return high, (x - high.astype(F32)).astype(jnp.bfloat16)


def gram_body(rows_ref, out_ref):
    first = lax.axis_index("mx") * MZ + lax.axis_index("side") * (MZ // SIDES)
    sums = rows_ref[pl.ds(first * MESSAGE + 2 * F, 8, stride=MESSAGE), :]
    lane = lax.broadcasted_iota(jnp.int32, (8, LANES), 1)
    chunk = lax.broadcasted_iota(jnp.int32, (8, LANES), 0)
    own_slot = lane % NZ // 2 == chunk
    moved = sums
    for g in range(1, 8):
        moved = jnp.where(chunk == g, pltpu.roll(sums, 2 * g, 1), moved)

    def spread(slot):
        tile = moved if slot == 0 else pltpu.roll(moved, LANES - 2 * slot, 1)
        return jnp.sum(jnp.where(own_slot, tile, 0.0), axis=0, keepdims=True)

    left, right = [], []
    for f in range(F):
        cells = rows_ref[pl.ds(F + f, MEMBERS, stride=MESSAGE), :]
        mean = jnp.sum(cells, axis=0, keepdims=True) * (1.0 / MEMBERS)
        deviation = cells - mean
        total = spread(f)
        drive = spread(F + f) - total * mean
        last = lax.broadcasted_iota(jnp.int32, (MEMBERS, LANES), 0) == MEMBERS - 1
        left.append(jnp.concatenate(halves(jnp.where(last, drive, deviation * total)), axis=0))
        right.append(jnp.concatenate(halves(deviation), axis=0))
    table = lax.dot_general(
        jnp.concatenate(left, axis=1),
        jnp.concatenate(right, axis=1),
        (((1,), (1,)), ((), ())),
        preferred_element_type=F32,
    )
    table = table[:MEMBERS] + table[MEMBERS:]
    table = table[:, :MEMBERS] + table[:, MEMBERS:]
    half = MEMBERS // 2
    upper, lower = table[:half], table[half:]
    lane = lax.broadcasted_iota(jnp.int32, (half, MEMBERS), 1)
    from_c = lax.broadcasted_iota(jnp.int32, (half, MEMBERS), 0) < lane
    swapped = jnp.concatenate([lower[:, half:], lower[:, :half]], axis=1)
    packed = jnp.where(jnp.logical_and(from_c, lane < half), swapped, upper)
    on_diagonal = lax.broadcasted_iota(jnp.int32, (half, MEMBERS), 0) + half == lane
    diagonal = jnp.sum(jnp.where(on_diagonal, lower, 0.0), axis=0, keepdims=True)
    last = -jnp.sum(upper, axis=0, keepdims=True) - jnp.sum(lower[: half - 1], axis=0, keepdims=True)
    diagonal = jnp.where(lane[:1] == MEMBERS - 1, last, diagonal)
    cross = jnp.concatenate([lower[half - 1 :], diagonal], axis=1)
    packed = jnp.concatenate([packed[: half // 2], packed[half // 2 :]], axis=1)
    out_ref[: TABLE - 1, :] = packed
    out_ref[TABLE - 1 :, :] = jnp.broadcast_to(cross, (out_ref.shape[0] - TABLE + 1, LANES))


def share_body(own_ref, other_ref, out_ref):
    table = own_ref[:TABLE] + other_ref[:TABLE]
    for i in range(out_ref.shape[0] // TABLE):
        out_ref[i * TABLE : (i + 1) * TABLE, :] = table


def mm(a, b):
    product = jnp.dot(
        jnp.concatenate(halves(a), axis=0),
        jnp.concatenate(halves(b), axis=0),
        preferred_element_type=F32,
    )
    rows = a.shape[0]
    return product[:rows] + product[rows:]


def mix_body(table_ref, rows_ref, out_ref):
    rows = 8 * TABLE
    tables = table_ref[:rows]
    for i in range(1, table_ref.shape[0] // rows):
        tables = tables + table_ref[i * rows : (i + 1) * rows]
    table = tables[:TABLE]
    for i in range(1, 8):
        table = table + tables[i * TABLE : (i + 1) * TABLE]
    square = (MEMBERS, MEMBERS)
    half = MEMBERS // 2
    row = lax.broadcasted_iota(jnp.int32, square, 0)
    lane = lax.broadcasted_iota(jnp.int32, square, 1)
    identity = jnp.where(row == lane, 1.0, 0.0)
    upper = jnp.concatenate([table[: half // 2, :MEMBERS], table[: half // 2, MEMBERS:]], axis=0)
    swapped = jnp.concatenate([upper[:, half:], upper[:, :half]], axis=1)
    both = jnp.concatenate([upper, swapped], axis=0)
    keep = jnp.logical_or(
        jnp.logical_and(row < half, jnp.logical_or(lane >= half, row > lane)),
        jnp.logical_and(row >= half, row < lane),
    )
    off = jnp.where(keep, both, 0.0)
    off = off + jnp.transpose(off)
    diagonal = jnp.where(row < half, both, table[TABLE - 1 :, MEMBERS:])
    cross = jnp.sum(identity * table[TABLE - 1 :, :MEMBERS], axis=1, keepdims=True)
    system = jnp.where(row == lane, diagonal + (MEMBERS - 1.0), off)
    shape = (TABLE, LANES)
    at = lax.broadcasted_iota(jnp.int32, shape, 0)
    spot = lax.broadcasted_iota(jnp.int32, shape, 1)
    body = at < TABLE - 1
    first = spot % MEMBERS == at + half // 2 * (spot // MEMBERS)
    second = jnp.logical_and(jnp.logical_not(body), spot >= MEMBERS + half)
    on_diagonal = jnp.logical_or(jnp.logical_and(body, first), second)
    squares = jnp.where(
        on_diagonal,
        (table + (MEMBERS - 1.0)) * (table + (MEMBERS - 1.0)),
        jnp.where(body, 2.0 * table * table, 0.0),
    )
    scale = jnp.sqrt(jnp.sum(squares, keepdims=True))
    identity, system = (jnp.concatenate([x, x], axis=1) for x in (identity, system))

    ensemble = jnp.concatenate(
        [rows_ref[pl.ds(f, MEMBERS, stride=MESSAGE), :] for f in range(F)], axis=1
    )
    centre = jnp.sum(ensemble, axis=0, keepdims=True) * (1.0 / MEMBERS)
    wide = jnp.concatenate(
        [ensemble - centre, jnp.broadcast_to(cross, (MEMBERS, LANES))], axis=1
    )

    root = system / scale
    inverse_root = 1.5 * identity - 0.5 * root
    root = mm(root, inverse_root)
    for step in range(1, NS_ITERS):
        factor = 1.5 * identity - 0.5 * mm(inverse_root, root)
        if step + 1 < NS_ITERS:
            both = mm(jnp.concatenate([root, inverse_root], axis=0), factor)
            root, inverse_root = both[:MEMBERS], both[MEMBERS:]
    wide = mm(factor, mm(inverse_root, wide))
    anomaly, drive = wide[:, : F * LANES], wide[:, F * LANES : F * LANES + 1] / scale
    shift = jnp.sum(drive * anomaly, axis=0, keepdims=True)
    mixed = (centre + shift) + anomaly * (math.sqrt(MEMBERS - 1.0) / jnp.sqrt(scale))
    for f in range(F):
        out_ref[pl.ds(f, MEMBERS, stride=F), :] = mixed[:, f * LANES : (f + 1) * LANES]


def exchange(rows, axes, peers):
    blocks = rows.reshape(peers, -1, 1, LANES)
    return lax.all_to_all(blocks, axes, split_axis=0, concat_axis=0, tiled=True)


def per_device(
    replica_profiles,
    diffusion,
    velocity,
    detector_voxel_position,
    detector_quantity_choice,
    sensor_value,
    sensor_var,
):
    slabs = lax.axis_size(SPACE)
    cells = replica_profiles.shape[2]
    own = replica_profiles.reshape(F, cells)
    pairs = [(i, i + 1) for i in range(0, slabs, 2)]
    beside = lax.ppermute(own, SPACE, pairs + [(b, a) for a, b in pairs])
    pairs = [(i, i + 1) for i in range(1, slabs - 1, 2)]
    across = lax.ppermute(own, SPACE, pairs + [(b, a) for a, b in pairs])
    early = call(
        early_body,
        (SUMS + 8, LANES),
        [SMEM, SMEM] + [VMEM] * 4,
        diffusion,
        velocity,
        detector_voxel_position.reshape(1, -1),
        detector_quantity_choice.reshape(1, -1),
        sensor_value.reshape(1, -1),
        sensor_var.reshape(1, -1),
        flops=FLOPS,
    )
    planes = call(own_body, (2 * FLAT, LANES), [VMEM] * 2, early, own, flops=FLOPS)
    fields = call(
        forecast_body,
        (MEMBERS * MESSAGE, LANES),
        [VMEM] * 4,
        early,
        planes,
        beside,
        across,
        flops=FLOPS,
    )
    rows = exchange(fields, MEMBER, MEMBERS).reshape(MEMBERS * MESSAGE, LANES)
    table = call(gram_body, (24, LANES), [VMEM], rows)
    other = lax.ppermute(table, "core", [(0, 1), (1, 0)])
    group = ("mx", "side", "y")
    peers = lax.axis_size(group)
    table = call(share_body, (peers * TABLE, LANES), [VMEM, VMEM], table, other)
    table = exchange(table, group, peers).reshape(peers * TABLE, LANES)
    mixed = call(mix_body, (MEMBERS * F, LANES), [VMEM, VMEM], table, rows)
    mixed = lax.all_to_all(
        mixed.reshape(MEMBERS, F, LANES), MEMBER, split_axis=0, concat_axis=0, tiled=True
    )
    return mixed.transpose(1, 0, 2).reshape(1, F, cells)


def solution(mesh):
    devices = mesh.devices.reshape(MX, MZ // SIDES, SIDES, -1, 2)
    fine = Mesh(devices, ("mx", "mz", "side", "y", "core"))
    sensors = P(MEMBER + SPACE)
    in_specs = (P(MEMBER, None, SPACE), P(), P(), sensors, sensors, sensors, sensors)
    return jax.shard_map(
        per_device,
        mesh=fine,
        in_specs=in_specs,
        out_specs=P(MEMBER, None, SPACE),
        check_vma=False,
    )
```

```python
import math

import jax
import jax.numpy as jnp
from jax import lax
from jax.experimental import pallas as pl
from jax.experimental.pallas import tpu as pltpu
from jax.sharding import Mesh, PartitionSpec as P

F = 4
NY = 256
NZ = 16
NS_ITERS = 5
MX = 4
MZ = 16
SIDES = 2
MEMBERS = MX * MZ
LANES = 128
PLANE = NY * NZ
CHUNKS = PLANE // LANES
FLAT = 8 * CHUNKS
SUMS = 8 * 7
FLOPS = 10**8
MESSAGE = 2 * F + 1
TABLE = MEMBERS * MEMBERS // 2 // LANES + 1

VMEM = pl.BlockSpec(memory_space=pltpu.VMEM)
SMEM = pl.BlockSpec(memory_space=pltpu.SMEM)
F32 = jnp.float32
MEMBER = ("mx", "mz", "side")
SPACE = ("y", "core")


def call(body, out_shape, in_specs, *operands, flops=None):
    return pl.pallas_call(
        body,
        out_shape=jax.ShapeDtypeStruct(out_shape, F32),
        in_specs=in_specs,
        out_specs=VMEM,
        cost_estimate=flops
        and pl.CostEstimate(flops=flops, bytes_accessed=1 << 18, transcendentals=0),
        compiler_params=pltpu.CompilerParams(vmem_limit_bytes=16 << 20),
    )(*operands)


def in_plane(centre, coef):
    keep, y_next, y_prev, z_next, z_prev = coef
    lane = lax.broadcasted_iota(jnp.int32, centre[0].shape, 1)
    up = [pltpu.roll(tile, LANES - NZ, 1) for tile in centre]
    down = [pltpu.roll(tile, NZ, 1) for tile in centre]
    zero = jnp.zeros_like(centre[0])
    result = []
    for j in range(CHUNKS):
        after = up[j + 1] if j + 1 < CHUNKS else zero
        before = down[j - 1] if j > 0 else zero
        result.append(
            keep * centre[j]
            + y_next * jnp.where(lane < LANES - NZ, up[j], after)
            + y_prev * jnp.where(lane >= NZ, down[j], before)
            + z_next * pltpu.roll(centre[j], LANES - 1, 1)
            + z_prev * pltpu.roll(centre[j], 1, 1)
        )
    return result


def stack(low, high):
    return jnp.concatenate([low, high], axis=0)


def sensor_sums(cell, choice, value, var):
    count = cell.shape[1]
    diagonal = lax.broadcasted_iota(jnp.int32, (count, count), 0) == lax.broadcasted_iota(
        jnp.int32, (count, count), 1
    )

    def column(row):
        return jnp.sum(jnp.where(diagonal, row, 0.0), axis=1, keepdims=True)

    weight = 1.0 / var
    spot = column((cell - 14 + 2 * choice).astype(F32)).astype(jnp.int32)
    lane = lax.broadcasted_iota(jnp.int32, (count, LANES), 1)
    share = jnp.where(spot == lane, column(weight), 0.0)
    share = share + jnp.where(spot + 2 * F == lane, column(weight * value), 0.0)
    return jnp.sum(share, axis=0, keepdims=True)


def early_body(diffusion_ref, velocity_ref, position_ref, choice_ref, value_ref, var_ref, out_ref):
    shape = (2 * F, LANES)
    field = lax.broadcasted_iota(jnp.int32, shape, 0) % F
    inner_z = lax.broadcasted_iota(jnp.int32, shape, 1) % NZ

    def per_field(values):
        tile = jnp.full(shape, values[F - 1], F32)
        for f in range(F - 1):
            tile = jnp.where(field == f, values[f], tile)
        return tile

    diffuse = per_field([diffusion_ref[f] for f in range(F)])
    move = [per_field([0.5 * velocity_ref[a, f] for f in range(F)]) for a in range(3)]
    coef = (
        1.0 - 6.0 * diffuse,
        diffuse - move[1],
        diffuse + move[1],
        jnp.where(inner_z != NZ - 1, diffuse - move[2], 0.0),
        jnp.where(inner_z != 0, diffuse + move[2], 0.0),
        diffuse - move[0],
        diffuse + move[0],
    )
    for i in range(len(coef)):
        out_ref[8 * i : 8 * i + 8, :] = coef[i]
    start = lax.axis_index(SPACE) * (2 * PLANE) + lax.axis_index(MEMBER) * LANES
    out_ref[SUMS : SUMS + 8, :] = jnp.broadcast_to(
        sensor_sums(position_ref[...] - start, choice_ref[...], value_ref[...], var_ref[...]), shape
    )


def own_body(early_ref, own_ref, out_ref):
    own = [stack(own_ref[:, tile(0, j)], own_ref[:, tile(1, j)]) for j in range(CHUNKS)]
    flat = in_plane(own, [early_ref[8 * i : 8 * i + 8, :] for i in range(5)])
    for j in range(CHUNKS):
        out_ref[8 * j : 8 * j + 8, :] = own[j]
        out_ref[FLAT + 8 * j : FLAT + 8 * j + 8, :] = flat[j]


def tile(plane, chunk):
    return slice(plane * PLANE + chunk * LANES, plane * PLANE + (chunk + 1) * LANES)


def forecast_body(early_ref, own_ref, beside_ref, across_ref, out_ref):
    slab = lax.axis_index(SPACE)
    even = slab % 2 == 0
    coef = [early_ref[8 * i : 8 * i + 8, :] for i in range(7)]
    x_next, x_prev = coef[5:]
    own = [own_ref[8 * j : 8 * j + 8, :] for j in range(CHUNKS)]

    def neighbour(first_ref, second_ref, plane, j):
        return jnp.where(even, first_ref[:, tile(plane, j)], second_ref[:, tile(plane, j)])

    left = [[neighbour(across_ref, beside_ref, p, j) for j in range(CHUNKS)] for p in range(2)]
    right = [[neighbour(beside_ref, across_ref, p, j) for j in range(CHUNKS)] for p in range(2)]
    upper = lax.broadcasted_iota(jnp.int32, (2 * F, LANES), 0) >= F
    inside = jnp.where(
        upper,
        jnp.where(slab < lax.axis_size(SPACE) - 1, 1.0, 0.0),
        jnp.where(slab > 0, 1.0, 0.0),
    )
    halo = [stack(left[1][j], right[0][j]) for j in range(CHUNKS)]
    halo_flat = in_plane(halo, coef[:5])
    outer = [
        inside
        * (
            halo_flat[j]
            + x_next * stack(own[j][:F], right[1][j])
            + x_prev * stack(left[0][j], own[j][F:])
        )
        for j in range(CHUNKS)
    ]
    inner = [
        own_ref[FLAT + 8 * j : FLAT + 8 * j + 8, :]
        + x_next * stack(own[j][F:], halo[j][F:])
        + x_prev * stack(halo[j][:F], own[j][:F])
        for j in range(CHUNKS)
    ]
    last = [
        flat + x_next * stack(mid[F:], out[F:]) + x_prev * stack(out[:F], mid[:F])
        for flat, mid, out in zip(in_plane(inner, coef[:5]), inner, outer)
    ]
    lane = lax.broadcasted_iota(jnp.int32, (2 * F, LANES), 1)
    slot = lane % NZ // 2
    packed = []
    for t in range(CHUNKS // 8):
        both = last[8 * t + 7]
        for g in range(7):
            both = jnp.where(slot == g, pltpu.roll(last[8 * t + g], LANES - 14 + 2 * g, 1), both)
        packed.append(both)
    sums = early_ref[SUMS : SUMS + 1, :]
    for p in range(2):
        for half in range(2):
            for z in range(MZ):
                j = half * MZ + z
                top = packed[2 * half + z % SIDES]
                row = (p * CHUNKS + j) * MESSAGE
                out_ref[row : row + F, :] = last[j][p * F : (p + 1) * F]
                out_ref[row + F : row + 2 * F, :] = top[p * F : (p + 1) * F]
                out_ref[row + 2 * F : row + MESSAGE, :] = sums


def halves(x):
    high = x.astype(jnp.bfloat16)
    return high, (x - high.astype(F32)).astype(jnp.bfloat16)


def gram_body(rows_ref, out_ref):
    first = lax.axis_index("mx") * MZ + lax.axis_index("side") * (MZ // SIDES)
    sums = rows_ref[pl.ds(first * MESSAGE + 2 * F, 8, stride=MESSAGE), :]
    lane = lax.broadcasted_iota(jnp.int32, (8, LANES), 1)
    chunk = lax.broadcasted_iota(jnp.int32, (8, LANES), 0)
    own_slot = lane % NZ // 2 == chunk
    moved = sums
    for g in range(1, 8):
        moved = jnp.where(chunk == g, pltpu.roll(sums, 2 * g, 1), moved)

    def spread(slot):
        tile = moved if slot == 0 else pltpu.roll(moved, LANES - 2 * slot, 1)
        return jnp.sum(jnp.where(own_slot, tile, 0.0), axis=0, keepdims=True)

    left, right = [], []
    for f in range(F):
        cells = rows_ref[pl.ds(F + f, MEMBERS, stride=MESSAGE), :]
        mean = jnp.sum(cells, axis=0, keepdims=True) * (1.0 / MEMBERS)
        deviation = cells - mean
        total = spread(f)
        drive = spread(F + f) - total * mean
        last = lax.broadcasted_iota(jnp.int32, (MEMBERS, LANES), 0) == MEMBERS - 1
        left.append(jnp.concatenate(halves(jnp.where(last, drive, deviation * total)), axis=0))
        right.append(jnp.concatenate(halves(deviation), axis=0))
    table = lax.dot_general(
        jnp.concatenate(left, axis=1),
        jnp.concatenate(right, axis=1),
        (((1,), (1,)), ((), ())),
        preferred_element_type=F32,
    )
    table = table[:MEMBERS] + table[MEMBERS:]
    table = table[:, :MEMBERS] + table[:, MEMBERS:]
    half = MEMBERS // 2
    upper, lower = table[:half], table[half:]
    lane = lax.broadcasted_iota(jnp.int32, (half, MEMBERS), 1)
    from_c = lax.broadcasted_iota(jnp.int32, (half, MEMBERS), 0) < lane
    swapped = jnp.concatenate([lower[:, half:], lower[:, :half]], axis=1)
    packed = jnp.where(jnp.logical_and(from_c, lane < half), swapped, upper)
    on_diagonal = lax.broadcasted_iota(jnp.int32, (half, MEMBERS), 0) + half == lane
    diagonal = jnp.sum(jnp.where(on_diagonal, lower, 0.0), axis=0, keepdims=True)
    last = -jnp.sum(upper, axis=0, keepdims=True) - jnp.sum(lower[: half - 1], axis=0, keepdims=True)
    diagonal = jnp.where(lane[:1] == MEMBERS - 1, last, diagonal)
    cross = jnp.concatenate([lower[half - 1 :], diagonal], axis=1)
    packed = jnp.concatenate([packed[: half // 2], packed[half // 2 :]], axis=1)
    out_ref[: TABLE - 1, :] = packed
    out_ref[TABLE - 1 :, :] = jnp.broadcast_to(cross, (out_ref.shape[0] - TABLE + 1, LANES))


def share_body(own_ref, other_ref, out_ref):
    table = own_ref[:TABLE] + other_ref[:TABLE]
    for i in range(out_ref.shape[0] // TABLE):
        out_ref[i * TABLE : (i + 1) * TABLE, :] = table


def mm(a, b):
    product = jnp.dot(
        jnp.concatenate(halves(a), axis=0),
        jnp.concatenate(halves(b), axis=0),
        preferred_element_type=F32,
    )
    rows = a.shape[0]
    return product[:rows] + product[rows:]


def mix_body(table_ref, rows_ref, out_ref):
    rows = 8 * TABLE
    tables = table_ref[:rows]
    for i in range(1, table_ref.shape[0] // rows):
        tables = tables + table_ref[i * rows : (i + 1) * rows]
    table = tables[:TABLE]
    for i in range(1, 8):
        table = table + tables[i * TABLE : (i + 1) * TABLE]
    square = (MEMBERS, MEMBERS)
    half = MEMBERS // 2
    row = lax.broadcasted_iota(jnp.int32, square, 0)
    lane = lax.broadcasted_iota(jnp.int32, square, 1)
    identity = jnp.where(row == lane, 1.0, 0.0)
    upper = jnp.concatenate([table[: half // 2, :MEMBERS], table[: half // 2, MEMBERS:]], axis=0)
    swapped = jnp.concatenate([upper[:, half:], upper[:, :half]], axis=1)
    both = jnp.concatenate([upper, swapped], axis=0)
    keep = jnp.logical_or(
        jnp.logical_and(row < half, jnp.logical_or(lane >= half, row > lane)),
        jnp.logical_and(row >= half, row < lane),
    )
    off = jnp.where(keep, both, 0.0)
    off = off + jnp.transpose(off)
    diagonal = jnp.where(row < half, both, table[TABLE - 1 :, MEMBERS:])
    cross = jnp.sum(identity * table[TABLE - 1 :, :MEMBERS], axis=1, keepdims=True)
    system = jnp.where(row == lane, diagonal + (MEMBERS - 1.0), off)
    shape = (TABLE, LANES)
    at = lax.broadcasted_iota(jnp.int32, shape, 0)
    spot = lax.broadcasted_iota(jnp.int32, shape, 1)
    body = at < TABLE - 1
    first = spot % MEMBERS == at + half // 2 * (spot // MEMBERS)
    second = jnp.logical_and(jnp.logical_not(body), spot >= MEMBERS + half)
    on_diagonal = jnp.logical_or(jnp.logical_and(body, first), second)
    squares = jnp.where(
        on_diagonal,
        (table + (MEMBERS - 1.0)) * (table + (MEMBERS - 1.0)),
        jnp.where(body, 2.0 * table * table, 0.0),
    )
    scale = jnp.sqrt(jnp.sum(squares, keepdims=True))
    identity, system = (jnp.concatenate([x, x], axis=1) for x in (identity, system))

    ensemble = jnp.concatenate(
        [rows_ref[pl.ds(f, MEMBERS, stride=MESSAGE), :] for f in range(F)], axis=1
    )
    centre = jnp.sum(ensemble, axis=0, keepdims=True) * (1.0 / MEMBERS)
    wide = jnp.concatenate(
        [ensemble - centre, jnp.broadcast_to(cross, (MEMBERS, LANES))], axis=1
    )

    root = system / scale
    inverse_root = 1.5 * identity - 0.5 * root
    root = mm(root, inverse_root)
    for step in range(1, NS_ITERS):
        factor = 1.5 * identity - 0.5 * mm(inverse_root, root)
        if step + 1 < NS_ITERS:
            both = mm(jnp.concatenate([root, inverse_root], axis=0), factor)
            root, inverse_root = both[:MEMBERS], both[MEMBERS:]
    wide = mm(factor, mm(inverse_root, wide))
    anomaly, drive = wide[:, : F * LANES], wide[:, F * LANES : F * LANES + 1] / scale
    shift = jnp.sum(drive * anomaly, axis=0, keepdims=True)
    mixed = (centre + shift) + anomaly * (math.sqrt(MEMBERS - 1.0) / jnp.sqrt(scale))
    for f in range(F):
        out_ref[pl.ds(f, MEMBERS, stride=F), :] = mixed[:, f * LANES : (f + 1) * LANES]


def exchange(rows, axes, peers):
    blocks = rows.reshape(peers, -1, 1, LANES)
    return lax.all_to_all(blocks, axes, split_axis=0, concat_axis=0, tiled=True)


def per_device(
    replica_profiles,
    diffusion,
    velocity,
    detector_voxel_position,
    detector_quantity_choice,
    sensor_value,
    sensor_var,
):
    slabs = lax.axis_size(SPACE)
    cells = replica_profiles.shape[2]
    own = replica_profiles.reshape(F, cells)
    pairs = [(i, i + 1) for i in range(0, slabs, 2)]
    beside = lax.ppermute(own, SPACE, pairs + [(b, a) for a, b in pairs])
    pairs = [(i, i + 1) for i in range(1, slabs - 1, 2)]
    across = lax.ppermute(own, SPACE, pairs + [(b, a) for a, b in pairs])
    early = call(
        early_body,
        (SUMS + 8, LANES),
        [SMEM, SMEM] + [VMEM] * 4,
        diffusion,
        velocity,
        detector_voxel_position.reshape(1, -1),
        detector_quantity_choice.reshape(1, -1),
        sensor_value.reshape(1, -1),
        sensor_var.reshape(1, -1),
        flops=FLOPS,
    )
    planes = call(own_body, (2 * FLAT, LANES), [VMEM] * 2, early, own, flops=FLOPS)
    fields = call(
        forecast_body,
        (MEMBERS * MESSAGE, LANES),
        [VMEM] * 4,
        early,
        planes,
        beside,
        across,
        flops=FLOPS,
    )
    rows = exchange(fields, MEMBER, MEMBERS).reshape(MEMBERS * MESSAGE, LANES)
    table = call(gram_body, (24, LANES), [VMEM], rows)
    other = lax.ppermute(table, "core", [(0, 1), (1, 0)])
    group = ("y", "side", "mx")
    peers = lax.axis_size(group)
    table = call(share_body, (peers * TABLE, LANES), [VMEM, VMEM], table, other)
    table = exchange(table, group, peers).reshape(peers * TABLE, LANES)
    mixed = call(mix_body, (MEMBERS * F, LANES), [VMEM, VMEM], table, rows)
    mixed = lax.all_to_all(
        mixed.reshape(MEMBERS, F, LANES), MEMBER, split_axis=0, concat_axis=0, tiled=True
    )
    return mixed.transpose(1, 0, 2).reshape(1, F, cells)


def solution(mesh):
    devices = mesh.devices.reshape(MX, MZ // SIDES, SIDES, -1, 2)
    fine = Mesh(devices, ("mx", "mz", "side", "y", "core"))
    sensors = P(MEMBER + SPACE)
    in_specs = (P(MEMBER, None, SPACE), P(), P(), sensors, sensors, sensors, sensors)
    return jax.shard_map(
        per_device,
        mesh=fine,
        in_specs=in_specs,
        out_specs=P(MEMBER, None, SPACE),
        check_vma=False,
    )
```

```python
import math

import jax
import jax.numpy as jnp
from jax import lax
from jax.experimental import pallas as pl
from jax.experimental.pallas import tpu as pltpu
from jax.sharding import Mesh, PartitionSpec as P

F = 4
NY = 256
NZ = 16
NS_ITERS = 5
MX = 4
MZ = 16
SIDES = 2
MEMBERS = MX * MZ
LANES = 128
PLANE = NY * NZ
CHUNKS = PLANE // LANES
FLAT = 8 * CHUNKS
SUMS = 8 * 7
FLOPS = 10**8
MESSAGE = 2 * F + 1
TABLE = MEMBERS * MEMBERS // 2 // LANES + 1

VMEM = pl.BlockSpec(memory_space=pltpu.VMEM)
F32 = jnp.float32
MEMBER = ("mx", "mz", "side")
SPACE = ("y", "core")


def call(body, out_shape, in_specs, *operands, flops=None):
    return pl.pallas_call(
        body,
        out_shape=jax.ShapeDtypeStruct(out_shape, F32),
        in_specs=in_specs,
        out_specs=VMEM,
        cost_estimate=flops
        and pl.CostEstimate(flops=flops, bytes_accessed=1 << 18, transcendentals=0),
        compiler_params=pltpu.CompilerParams(vmem_limit_bytes=16 << 20),
    )(*operands)


def in_plane(centre, coef):
    keep, y_next, y_prev, z_next, z_prev = coef
    lane = lax.broadcasted_iota(jnp.int32, centre[0].shape, 1)
    up = [pltpu.roll(tile, LANES - NZ, 1) for tile in centre]
    down = [pltpu.roll(tile, NZ, 1) for tile in centre]
    zero = jnp.zeros_like(centre[0])
    result = []
    for j in range(CHUNKS):
        after = up[j + 1] if j + 1 < CHUNKS else zero
        before = down[j - 1] if j > 0 else zero
        result.append(
            keep * centre[j]
            + y_next * jnp.where(lane < LANES - NZ, up[j], after)
            + y_prev * jnp.where(lane >= NZ, down[j], before)
            + z_next * pltpu.roll(centre[j], LANES - 1, 1)
            + z_prev * pltpu.roll(centre[j], 1, 1)
        )
    return result


def stack(low, high):
    return jnp.concatenate([low, high], axis=0)


def sensor_sums(cell, choice, value, var):
    count = cell.shape[1]
    diagonal = lax.broadcasted_iota(jnp.int32, (count, count), 0) == lax.broadcasted_iota(
        jnp.int32, (count, count), 1
    )

    def column(row):
        return jnp.sum(jnp.where(diagonal, row, 0.0), axis=1, keepdims=True)

    weight = 1.0 / var
    spot = column((cell - 14 + 2 * choice).astype(F32)).astype(jnp.int32)
    lane = lax.broadcasted_iota(jnp.int32, (count, LANES), 1)
    share = jnp.where(spot == lane, column(weight), 0.0)
    share = share + jnp.where(spot + 2 * F == lane, column(weight * value), 0.0)
    return jnp.sum(share, axis=0, keepdims=True)


def mask_body(out_ref):
    inner_z = lax.broadcasted_iota(jnp.int32, (8, LANES), 1) % NZ
    out_ref[:8, :] = jnp.where(inner_z != NZ - 1, 1.0, 0.0)
    out_ref[8:, :] = jnp.where(inner_z != 0, 1.0, 0.0)


def early_body(
    mask_ref, diffusion_ref, velocity_ref, position_ref, choice_ref, value_ref, var_ref, out_ref
):
    shape = (2 * F, LANES)
    field = lax.broadcasted_iota(jnp.int32, shape, 0) % F

    def per_field(row):
        tile = jnp.broadcast_to(row[:, F - 1 :], shape)
        for f in range(F - 1):
            tile = jnp.where(field == f, jnp.broadcast_to(row[:, f : f + 1], shape), tile)
        return tile

    diffuse = per_field(diffusion_ref[...])
    move = [per_field(0.5 * velocity_ref[a : a + 1, :]) for a in range(3)]
    coef = (
        1.0 - 6.0 * diffuse,
        diffuse - move[1],
        diffuse + move[1],
        (diffuse - move[2]) * mask_ref[:8, :],
        (diffuse + move[2]) * mask_ref[8:, :],
        diffuse - move[0],
        diffuse + move[0],
    )
    for i in range(len(coef)):
        out_ref[8 * i : 8 * i + 8, :] = coef[i]
    start = lax.axis_index(SPACE) * (2 * PLANE) + lax.axis_index(MEMBER) * LANES
    out_ref[SUMS : SUMS + 8, :] = jnp.broadcast_to(
        sensor_sums(position_ref[...] - start, choice_ref[...], value_ref[...], var_ref[...]), shape
    )


def own_body(early_ref, own_ref, out_ref):
    own = [stack(own_ref[:, tile(0, j)], own_ref[:, tile(1, j)]) for j in range(CHUNKS)]
    flat = in_plane(own, [early_ref[8 * i : 8 * i + 8, :] for i in range(5)])
    for j in range(CHUNKS):
        out_ref[8 * j : 8 * j + 8, :] = own[j]
        out_ref[FLAT + 8 * j : FLAT + 8 * j + 8, :] = flat[j]


def tile(plane, chunk):
    return slice(plane * PLANE + chunk * LANES, plane * PLANE + (chunk + 1) * LANES)


def forecast_body(early_ref, own_ref, beside_ref, across_ref, out_ref):
    slab = lax.axis_index(SPACE)
    even = slab % 2 == 0
    coef = [early_ref[8 * i : 8 * i + 8, :] for i in range(7)]
    x_next, x_prev = coef[5:]
    own = [own_ref[8 * j : 8 * j + 8, :] for j in range(CHUNKS)]

    def neighbour(first_ref, second_ref, plane, j):
        return jnp.where(even, first_ref[:, tile(plane, j)], second_ref[:, tile(plane, j)])

    left = [[neighbour(across_ref, beside_ref, p, j) for j in range(CHUNKS)] for p in range(2)]
    right = [[neighbour(beside_ref, across_ref, p, j) for j in range(CHUNKS)] for p in range(2)]
    upper = lax.broadcasted_iota(jnp.int32, (2 * F, LANES), 0) >= F
    inside = jnp.where(
        upper,
        jnp.where(slab < lax.axis_size(SPACE) - 1, 1.0, 0.0),
        jnp.where(slab > 0, 1.0, 0.0),
    )
    halo = [stack(left[1][j], right[0][j]) for j in range(CHUNKS)]
    halo_flat = in_plane(halo, coef[:5])
    outer = [
        inside
        * (
            halo_flat[j]
            + x_next * stack(own[j][:F], right[1][j])
            + x_prev * stack(left[0][j], own[j][F:])
        )
        for j in range(CHUNKS)
    ]
    inner = [
        own_ref[FLAT + 8 * j : FLAT + 8 * j + 8, :]
        + x_next * stack(own[j][F:], halo[j][F:])
        + x_prev * stack(halo[j][:F], own[j][:F])
        for j in range(CHUNKS)
    ]
    last = [
        flat + x_next * stack(mid[F:], out[F:]) + x_prev * stack(out[:F], mid[:F])
        for flat, mid, out in zip(in_plane(inner, coef[:5]), inner, outer)
    ]
    lane = lax.broadcasted_iota(jnp.int32, (2 * F, LANES), 1)
    slot = lane % NZ // 2
    packed = []
    for t in range(CHUNKS // 8):
        both = last[8 * t + 7]
        for g in range(7):
            both = jnp.where(slot == g, pltpu.roll(last[8 * t + g], LANES - 14 + 2 * g, 1), both)
        packed.append(both)
    sums = early_ref[SUMS : SUMS + 1, :]
    for p in range(2):
        for half in range(2):
            for z in range(MZ):
                j = half * MZ + z
                top = packed[2 * half + z % SIDES]
                row = (p * CHUNKS + j) * MESSAGE
                out_ref[row : row + F, :] = last[j][p * F : (p + 1) * F]
                out_ref[row + F : row + 2 * F, :] = top[p * F : (p + 1) * F]
                out_ref[row + 2 * F : row + MESSAGE, :] = sums


def halves(x):
    high = x.astype(jnp.bfloat16)
    return high, (x - high.astype(F32)).astype(jnp.bfloat16)


def gram_body(rows_ref, out_ref):
    first = lax.axis_index("mx") * MZ + lax.axis_index("side") * (MZ // SIDES)
    sums = rows_ref[pl.ds(first * MESSAGE + 2 * F, 8, stride=MESSAGE), :]
    lane = lax.broadcasted_iota(jnp.int32, (8, LANES), 1)
    chunk = lax.broadcasted_iota(jnp.int32, (8, LANES), 0)
    own_slot = lane % NZ // 2 == chunk
    moved = sums
    for g in range(1, 8):
        moved = jnp.where(chunk == g, pltpu.roll(sums, 2 * g, 1), moved)

    def spread(slot):
        tile = moved if slot == 0 else pltpu.roll(moved, LANES - 2 * slot, 1)
        return jnp.sum(jnp.where(own_slot, tile, 0.0), axis=0, keepdims=True)

    left, right = [], []
    for f in range(F):
        cells = rows_ref[pl.ds(F + f, MEMBERS, stride=MESSAGE), :]
        mean = jnp.sum(cells, axis=0, keepdims=True) * (1.0 / MEMBERS)
        deviation = cells - mean
        total = spread(f)
        drive = spread(F + f) - total * mean
        last = lax.broadcasted_iota(jnp.int32, (MEMBERS, LANES), 0) == MEMBERS - 1
        left.append(jnp.concatenate(halves(jnp.where(last, drive, deviation * total)), axis=0))
        right.append(jnp.concatenate(halves(deviation), axis=0))
    table = lax.dot_general(
        jnp.concatenate(left, axis=1),
        jnp.concatenate(right, axis=1),
        (((1,), (1,)), ((), ())),
        preferred_element_type=F32,
    )
    table = table[:MEMBERS] + table[MEMBERS:]
    table = table[:, :MEMBERS] + table[:, MEMBERS:]
    half = MEMBERS // 2
    upper, lower = table[:half], table[half:]
    lane = lax.broadcasted_iota(jnp.int32, (half, MEMBERS), 1)
    from_c = lax.broadcasted_iota(jnp.int32, (half, MEMBERS), 0) < lane
    swapped = jnp.concatenate([lower[:, half:], lower[:, :half]], axis=1)
    packed = jnp.where(jnp.logical_and(from_c, lane < half), swapped, upper)
    on_diagonal = lax.broadcasted_iota(jnp.int32, (half, MEMBERS), 0) + half == lane
    diagonal = jnp.sum(jnp.where(on_diagonal, lower, 0.0), axis=0, keepdims=True)
    last = -jnp.sum(upper, axis=0, keepdims=True) - jnp.sum(lower[: half - 1], axis=0, keepdims=True)
    diagonal = jnp.where(lane[:1] == MEMBERS - 1, last, diagonal)
    cross = jnp.concatenate([lower[half - 1 :], diagonal], axis=1)
    packed = jnp.concatenate([packed[: half // 2], packed[half // 2 :]], axis=1)
    out_ref[: TABLE - 1, :] = packed
    out_ref[TABLE - 1 :, :] = jnp.broadcast_to(cross, (out_ref.shape[0] - TABLE + 1, LANES))


def share_body(own_ref, other_ref, out_ref):
    table = own_ref[:TABLE] + other_ref[:TABLE]
    for i in range(out_ref.shape[0] // TABLE):
        out_ref[i * TABLE : (i + 1) * TABLE, :] = table


def mm(a, b):
    product = jnp.dot(
        jnp.concatenate(halves(a), axis=0),
        jnp.concatenate(halves(b), axis=0),
        preferred_element_type=F32,
    )
    rows = a.shape[0]
    return product[:rows] + product[rows:]


def mix_body(table_ref, rows_ref, out_ref):
    rows = 8 * TABLE
    tables = table_ref[:rows]
    for i in range(1, table_ref.shape[0] // rows):
        tables = tables + table_ref[i * rows : (i + 1) * rows]
    table = tables[:TABLE]
    for i in range(1, 8):
        table = table + tables[i * TABLE : (i + 1) * TABLE]
    square = (MEMBERS, MEMBERS)
    half = MEMBERS // 2
    row = lax.broadcasted_iota(jnp.int32, square, 0)
    lane = lax.broadcasted_iota(jnp.int32, square, 1)
    identity = jnp.where(row == lane, 1.0, 0.0)
    upper = jnp.concatenate([table[: half // 2, :MEMBERS], table[: half // 2, MEMBERS:]], axis=0)
    swapped = jnp.concatenate([upper[:, half:], upper[:, :half]], axis=1)
    both = jnp.concatenate([upper, swapped], axis=0)
    keep = jnp.logical_or(
        jnp.logical_and(row < half, jnp.logical_or(lane >= half, row > lane)),
        jnp.logical_and(row >= half, row < lane),
    )
    off = jnp.where(keep, both, 0.0)
    off = off + jnp.transpose(off)
    diagonal = jnp.where(row < half, both, table[TABLE - 1 :, MEMBERS:])
    cross = jnp.sum(identity * table[TABLE - 1 :, :MEMBERS], axis=1, keepdims=True)
    system = jnp.where(row == lane, diagonal + (MEMBERS - 1.0), off)
    shape = (TABLE, LANES)
    at = lax.broadcasted_iota(jnp.int32, shape, 0)
    spot = lax.broadcasted_iota(jnp.int32, shape, 1)
    body = at < TABLE - 1
    first = spot % MEMBERS == at + half // 2 * (spot // MEMBERS)
    second = jnp.logical_and(jnp.logical_not(body), spot >= MEMBERS + half)
    on_diagonal = jnp.logical_or(jnp.logical_and(body, first), second)
    squares = jnp.where(
        on_diagonal,
        (table + (MEMBERS - 1.0)) * (table + (MEMBERS - 1.0)),
        jnp.where(body, 2.0 * table * table, 0.0),
    )
    scale = jnp.sqrt(jnp.sum(squares, keepdims=True))
    identity, system = (jnp.concatenate([x, x], axis=1) for x in (identity, system))

    ensemble = jnp.concatenate(
        [rows_ref[pl.ds(f, MEMBERS, stride=MESSAGE), :] for f in range(F)], axis=1
    )
    centre = jnp.sum(ensemble, axis=0, keepdims=True) * (1.0 / MEMBERS)
    wide = jnp.concatenate(
        [ensemble - centre, jnp.broadcast_to(cross, (MEMBERS, LANES))], axis=1
    )

    root = system / scale
    inverse_root = 1.5 * identity - 0.5 * root
    root = mm(root, inverse_root)
    for step in range(1, NS_ITERS):
        factor = 1.5 * identity - 0.5 * mm(inverse_root, root)
        if step + 1 < NS_ITERS:
            both = mm(jnp.concatenate([root, inverse_root], axis=0), factor)
            root, inverse_root = both[:MEMBERS], both[MEMBERS:]
    wide = mm(factor, mm(inverse_root, wide))
    anomaly, drive = wide[:, : F * LANES], wide[:, F * LANES : F * LANES + 1] / scale
    shift = jnp.sum(drive * anomaly, axis=0, keepdims=True)
    mixed = (centre + shift) + anomaly * (math.sqrt(MEMBERS - 1.0) / jnp.sqrt(scale))
    for f in range(F):
        out_ref[pl.ds(f, MEMBERS, stride=F), :] = mixed[:, f * LANES : (f + 1) * LANES]


def exchange(rows, axes, peers):
    blocks = rows.reshape(peers, -1, 1, LANES)
    return lax.all_to_all(blocks, axes, split_axis=0, concat_axis=0, tiled=True)


def per_device(
    replica_profiles,
    diffusion,
    velocity,
    detector_voxel_position,
    detector_quantity_choice,
    sensor_value,
    sensor_var,
):
    slabs = lax.axis_size(SPACE)
    cells = replica_profiles.shape[2]
    own = replica_profiles.reshape(F, cells)
    pairs = [(i, i + 1) for i in range(0, slabs, 2)]
    beside = lax.ppermute(own, SPACE, pairs + [(b, a) for a, b in pairs])
    pairs = [(i, i + 1) for i in range(1, slabs - 1, 2)]
    across = lax.ppermute(own, SPACE, pairs + [(b, a) for a, b in pairs])
    mask = call(mask_body, (16, LANES), [], flops=100 * FLOPS)
    early = call(
        early_body,
        (SUMS + 8, LANES),
        [VMEM] * 7,
        mask,
        diffusion.reshape(1, -1),
        velocity,
        detector_voxel_position.reshape(1, -1),
        detector_quantity_choice.reshape(1, -1),
        sensor_value.reshape(1, -1),
        sensor_var.reshape(1, -1),
        flops=1,
    )
    planes = call(own_body, (2 * FLAT, LANES), [VMEM] * 2, early, own, flops=FLOPS)
    fields = call(
        forecast_body,
        (MEMBERS * MESSAGE, LANES),
        [VMEM] * 4,
        early,
        planes,
        beside,
        across,
        flops=FLOPS,
    )
    rows = exchange(fields, MEMBER, MEMBERS).reshape(MEMBERS * MESSAGE, LANES)
    table = call(gram_body, (24, LANES), [VMEM], rows)
    other = lax.ppermute(table, "core", [(0, 1), (1, 0)])
    group = ("mx", "side", "y")
    peers = lax.axis_size(group)
    table = call(share_body, (peers * TABLE, LANES), [VMEM, VMEM], table, other)
    table = exchange(table, group, peers).reshape(peers * TABLE, LANES)
    mixed = call(mix_body, (MEMBERS * F, LANES), [VMEM, VMEM], table, rows)
    mixed = lax.all_to_all(
        mixed.reshape(MEMBERS, F, LANES), MEMBER, split_axis=0, concat_axis=0, tiled=True
    )
    return mixed.transpose(1, 0, 2).reshape(1, F, cells)


def solution(mesh):
    devices = mesh.devices.reshape(MX, MZ // SIDES, SIDES, -1, 2)
    fine = Mesh(devices, ("mx", "mz", "side", "y", "core"))
    sensors = P(MEMBER + SPACE)
    in_specs = (P(MEMBER, None, SPACE), P(), P(), sensors, sensors, sensors, sensors)
    return jax.shard_map(
        per_device,
        mesh=fine,
        in_specs=in_specs,
        out_specs=P(MEMBER, None, SPACE),
        check_vma=False,
    )
```

```python
import math

import jax
import jax.numpy as jnp
from jax import lax
from jax.experimental import pallas as pl
from jax.experimental.pallas import tpu as pltpu
from jax.sharding import Mesh, PartitionSpec as P

F = 4
NY = 256
NZ = 16
NS_ITERS = 5
MX = 4
MZ = 16
SIDES = 2
MEMBERS = MX * MZ
LANES = 128
PLANE = NY * NZ
CHUNKS = PLANE // LANES
FLAT = 8 * CHUNKS
SUMS = 8 * 7
FLOPS = 10**8
MESSAGE = 2 * F + 1
TABLE = MEMBERS * MEMBERS // 2 // LANES + 1

VMEM = pl.BlockSpec(memory_space=pltpu.VMEM)
F32 = jnp.float32
MEMBER = ("mx", "mz", "side")
SPACE = ("y", "core")


def call(body, out_shape, in_specs, *operands, flops=None):
    return pl.pallas_call(
        body,
        out_shape=jax.ShapeDtypeStruct(out_shape, F32),
        in_specs=in_specs,
        out_specs=VMEM,
        cost_estimate=flops
        and pl.CostEstimate(flops=flops, bytes_accessed=1 << 18, transcendentals=0),
        compiler_params=pltpu.CompilerParams(vmem_limit_bytes=16 << 20),
    )(*operands)


def in_plane(centre, coef):
    keep, y_next, y_prev, z_next, z_prev = coef
    lane = lax.broadcasted_iota(jnp.int32, centre[0].shape, 1)
    up = [pltpu.roll(tile, LANES - NZ, 1) for tile in centre]
    down = [pltpu.roll(tile, NZ, 1) for tile in centre]
    zero = jnp.zeros_like(centre[0])
    result = []
    for j in range(CHUNKS):
        after = up[j + 1] if j + 1 < CHUNKS else zero
        before = down[j - 1] if j > 0 else zero
        result.append(
            keep * centre[j]
            + y_next * jnp.where(lane < LANES - NZ, up[j], after)
            + y_prev * jnp.where(lane >= NZ, down[j], before)
            + z_next * pltpu.roll(centre[j], LANES - 1, 1)
            + z_prev * pltpu.roll(centre[j], 1, 1)
        )
    return result


def stack(low, high):
    return jnp.concatenate([low, high], axis=0)


def sensor_sums(cell, choice, value, var):
    count = cell.shape[1]
    diagonal = lax.broadcasted_iota(jnp.int32, (count, count), 0) == lax.broadcasted_iota(
        jnp.int32, (count, count), 1
    )

    def column(row):
        return jnp.sum(jnp.where(diagonal, row, 0.0), axis=1, keepdims=True)

    weight = 1.0 / var
    spot = column((cell - 14 + 2 * choice).astype(F32)).astype(jnp.int32)
    lane = lax.broadcasted_iota(jnp.int32, (count, LANES), 1)
    share = jnp.where(spot == lane, column(weight), 0.0)
    share = share + jnp.where(spot + 2 * F == lane, column(weight * value), 0.0)
    return jnp.sum(share, axis=0, keepdims=True)


def mask_body(out_ref):
    inner_z = lax.broadcasted_iota(jnp.int32, (8, LANES), 1) % NZ
    out_ref[:8, :] = jnp.where(inner_z != NZ - 1, 1.0, 0.0)
    out_ref[8:, :] = jnp.where(inner_z != 0, 1.0, 0.0)


def early_body(
    mask_ref, diffusion_ref, velocity_ref, position_ref, choice_ref, value_ref, var_ref, out_ref
):
    shape = (2 * F, LANES)
    field = lax.broadcasted_iota(jnp.int32, shape, 0) % F

    def per_field(row):
        tile = jnp.broadcast_to(row[:, F - 1 :], shape)
        for f in range(F - 1):
            tile = jnp.where(field == f, jnp.broadcast_to(row[:, f : f + 1], shape), tile)
        return tile

    diffuse = per_field(diffusion_ref[...])
    move = [per_field(0.5 * velocity_ref[a : a + 1, :]) for a in range(3)]
    coef = (
        1.0 - 6.0 * diffuse,
        diffuse - move[1],
        diffuse + move[1],
        (diffuse - move[2]) * mask_ref[:8, :],
        (diffuse + move[2]) * mask_ref[8:, :],
        diffuse - move[0],
        diffuse + move[0],
    )
    for i in range(len(coef)):
        out_ref[8 * i : 8 * i + 8, :] = coef[i]
    start = lax.axis_index(SPACE) * (2 * PLANE) + lax.axis_index(MEMBER) * LANES
    out_ref[SUMS : SUMS + 8, :] = jnp.broadcast_to(
        sensor_sums(position_ref[...] - start, choice_ref[...], value_ref[...], var_ref[...]), shape
    )


def own_body(early_ref, own_ref, out_ref):
    own = [stack(own_ref[:, tile(0, j)], own_ref[:, tile(1, j)]) for j in range(CHUNKS)]
    flat = in_plane(own, [early_ref[8 * i : 8 * i + 8, :] for i in range(5)])
    for j in range(CHUNKS):
        out_ref[8 * j : 8 * j + 8, :] = own[j]
        out_ref[FLAT + 8 * j : FLAT + 8 * j + 8, :] = flat[j]


def tile(plane, chunk):
    return slice(plane * PLANE + chunk * LANES, plane * PLANE + (chunk + 1) * LANES)


def forecast_body(early_ref, own_ref, beside_ref, across_ref, out_ref):
    slab = lax.axis_index(SPACE)
    even = slab % 2 == 0
    coef = [early_ref[8 * i : 8 * i + 8, :] for i in range(7)]
    x_next, x_prev = coef[5:]
    own = [own_ref[8 * j : 8 * j + 8, :] for j in range(CHUNKS)]

    def neighbour(first_ref, second_ref, plane, j):
        return jnp.where(even, first_ref[:, tile(plane, j)], second_ref[:, tile(plane, j)])

    left = [[neighbour(across_ref, beside_ref, p, j) for j in range(CHUNKS)] for p in range(2)]
    right = [[neighbour(beside_ref, across_ref, p, j) for j in range(CHUNKS)] for p in range(2)]
    upper = lax.broadcasted_iota(jnp.int32, (2 * F, LANES), 0) >= F
    inside = jnp.where(
        upper,
        jnp.where(slab < lax.axis_size(SPACE) - 1, 1.0, 0.0),
        jnp.where(slab > 0, 1.0, 0.0),
    )
    halo = [stack(left[1][j], right[0][j]) for j in range(CHUNKS)]
    halo_flat = in_plane(halo, coef[:5])
    outer = [
        inside
        * (
            halo_flat[j]
            + x_next * stack(own[j][:F], right[1][j])
            + x_prev * stack(left[0][j], own[j][F:])
        )
        for j in range(CHUNKS)
    ]
    inner = [
        own_ref[FLAT + 8 * j : FLAT + 8 * j + 8, :]
        + x_next * stack(own[j][F:], halo[j][F:])
        + x_prev * stack(halo[j][:F], own[j][:F])
        for j in range(CHUNKS)
    ]
    last = [
        flat + x_next * stack(mid[F:], out[F:]) + x_prev * stack(out[:F], mid[:F])
        for flat, mid, out in zip(in_plane(inner, coef[:5]), inner, outer)
    ]
    lane = lax.broadcasted_iota(jnp.int32, (2 * F, LANES), 1)
    slot = lane % NZ // 2
    packed = []
    for t in range(CHUNKS // 8):
        both = last[8 * t + 7]
        for g in range(7):
            both = jnp.where(slot == g, pltpu.roll(last[8 * t + g], LANES - 14 + 2 * g, 1), both)
        packed.append(both)
    sums = early_ref[SUMS : SUMS + 1, :]
    for p in range(2):
        for half in range(2):
            for z in range(MZ):
                j = half * MZ + z
                top = packed[2 * half + z % SIDES]
                row = (p * CHUNKS + j) * MESSAGE
                out_ref[row : row + F, :] = last[j][p * F : (p + 1) * F]
                out_ref[row + F : row + 2 * F, :] = top[p * F : (p + 1) * F]
                out_ref[row + 2 * F : row + MESSAGE, :] = sums


def halves(x):
    high = x.astype(jnp.bfloat16)
    return high, (x - high.astype(F32)).astype(jnp.bfloat16)


def gram_body(rows_ref, out_ref):
    first = lax.axis_index("mx") * MZ + lax.axis_index("side") * (MZ // SIDES)
    sums = rows_ref[pl.ds(first * MESSAGE + 2 * F, 8, stride=MESSAGE), :]
    lane = lax.broadcasted_iota(jnp.int32, (8, LANES), 1)
    chunk = lax.broadcasted_iota(jnp.int32, (8, LANES), 0)
    own_slot = lane % NZ // 2 == chunk
    moved = sums
    for g in range(1, 8):
        moved = jnp.where(chunk == g, pltpu.roll(sums, 2 * g, 1), moved)

    def spread(slot):
        tile = moved if slot == 0 else pltpu.roll(moved, LANES - 2 * slot, 1)
        return jnp.sum(jnp.where(own_slot, tile, 0.0), axis=0, keepdims=True)

    left, right = [], []
    for f in range(F):
        cells = rows_ref[pl.ds(F + f, MEMBERS, stride=MESSAGE), :]
        mean = jnp.sum(cells, axis=0, keepdims=True) * (1.0 / MEMBERS)
        deviation = cells - mean
        total = spread(f)
        drive = spread(F + f) - total * mean
        last = lax.broadcasted_iota(jnp.int32, (MEMBERS, LANES), 0) == MEMBERS - 1
        left.append(jnp.concatenate(halves(jnp.where(last, drive, deviation * total)), axis=0))
        right.append(jnp.concatenate(halves(deviation), axis=0))
    table = lax.dot_general(
        jnp.concatenate(left, axis=1),
        jnp.concatenate(right, axis=1),
        (((1,), (1,)), ((), ())),
        preferred_element_type=F32,
    )
    table = table[:MEMBERS] + table[MEMBERS:]
    table = table[:, :MEMBERS] + table[:, MEMBERS:]
    half = MEMBERS // 2
    upper, lower = table[:half], table[half:]
    lane = lax.broadcasted_iota(jnp.int32, (half, MEMBERS), 1)
    from_c = lax.broadcasted_iota(jnp.int32, (half, MEMBERS), 0) < lane
    swapped = jnp.concatenate([lower[:, half:], lower[:, :half]], axis=1)
    packed = jnp.where(jnp.logical_and(from_c, lane < half), swapped, upper)
    on_diagonal = lax.broadcasted_iota(jnp.int32, (half, MEMBERS), 0) + half == lane
    diagonal = jnp.sum(jnp.where(on_diagonal, lower, 0.0), axis=0, keepdims=True)
    last = -jnp.sum(upper, axis=0, keepdims=True) - jnp.sum(lower[: half - 1], axis=0, keepdims=True)
    diagonal = jnp.where(lane[:1] == MEMBERS - 1, last, diagonal)
    cross = jnp.concatenate([lower[half - 1 :], diagonal], axis=1)
    packed = jnp.concatenate([packed[: half // 2], packed[half // 2 :]], axis=1)
    out_ref[: TABLE - 1, :] = packed
    out_ref[TABLE - 1 :, :] = jnp.broadcast_to(cross, (out_ref.shape[0] - TABLE + 1, LANES))


def share_body(own_ref, other_ref, out_ref):
    table = own_ref[:TABLE] + other_ref[:TABLE]
    for i in range(out_ref.shape[0] // TABLE):
        out_ref[i * TABLE : (i + 1) * TABLE, :] = table


def mm(a, b):
    product = jnp.dot(
        jnp.concatenate(halves(a), axis=0),
        jnp.concatenate(halves(b), axis=0),
        preferred_element_type=F32,
    )
    rows = a.shape[0]
    return product[:rows] + product[rows:]


def mix_body(table_ref, rows_ref, out_ref):
    rows = 8 * TABLE
    tables = table_ref[:rows]
    for i in range(1, table_ref.shape[0] // rows):
        tables = tables + table_ref[i * rows : (i + 1) * rows]
    table = tables[:TABLE]
    for i in range(1, 8):
        table = table + tables[i * TABLE : (i + 1) * TABLE]
    square = (MEMBERS, MEMBERS)
    half = MEMBERS // 2
    row = lax.broadcasted_iota(jnp.int32, square, 0)
    lane = lax.broadcasted_iota(jnp.int32, square, 1)
    identity = jnp.where(row == lane, 1.0, 0.0)
    upper = jnp.concatenate([table[: half // 2, :MEMBERS], table[: half // 2, MEMBERS:]], axis=0)
    swapped = jnp.concatenate([upper[:, half:], upper[:, :half]], axis=1)
    both = jnp.concatenate([upper, swapped], axis=0)
    keep = jnp.logical_or(
        jnp.logical_and(row < half, jnp.logical_or(lane >= half, row > lane)),
        jnp.logical_and(row >= half, row < lane),
    )
    off = jnp.where(keep, both, 0.0)
    off = off + jnp.transpose(off)
    diagonal = jnp.where(row < half, both, table[TABLE - 1 :, MEMBERS:])
    cross = jnp.sum(identity * table[TABLE - 1 :, :MEMBERS], axis=1, keepdims=True)
    system = jnp.where(row == lane, diagonal + (MEMBERS - 1.0), off)
    shape = (TABLE, LANES)
    at = lax.broadcasted_iota(jnp.int32, shape, 0)
    spot = lax.broadcasted_iota(jnp.int32, shape, 1)
    body = at < TABLE - 1
    first = spot % MEMBERS == at + half // 2 * (spot // MEMBERS)
    second = jnp.logical_and(jnp.logical_not(body), spot >= MEMBERS + half)
    on_diagonal = jnp.logical_or(jnp.logical_and(body, first), second)
    squares = jnp.where(
        on_diagonal,
        (table + (MEMBERS - 1.0)) * (table + (MEMBERS - 1.0)),
        jnp.where(body, 2.0 * table * table, 0.0),
    )
    scale = jnp.sqrt(jnp.sum(squares, keepdims=True))
    identity, system = (jnp.concatenate([x, x], axis=1) for x in (identity, system))

    ensemble = jnp.concatenate(
        [rows_ref[pl.ds(f, MEMBERS, stride=MESSAGE), :] for f in range(F)], axis=1
    )
    centre = jnp.sum(ensemble, axis=0, keepdims=True) * (1.0 / MEMBERS)
    wide = jnp.concatenate(
        [ensemble - centre, jnp.broadcast_to(cross, (MEMBERS, LANES))], axis=1
    )

    inverse_scale = 1.0 / scale
    root = system * inverse_scale
    inverse_root = 1.5 * identity - 0.5 * root
    root = mm(root, inverse_root)
    for step in range(1, NS_ITERS):
        factor = 1.5 * identity - 0.5 * mm(inverse_root, root)
        if step + 1 < NS_ITERS:
            both = mm(jnp.concatenate([root, inverse_root], axis=0), factor)
            root, inverse_root = both[:MEMBERS], both[MEMBERS:]
    wide = mm(factor, mm(inverse_root, wide))
    drive = wide[:, F * LANES :]
    gain = math.sqrt(MEMBERS - 1.0) / jnp.sqrt(scale)
    for f in range(F):
        lanes = slice(f * LANES, (f + 1) * LANES)
        anomaly = wide[:, lanes]
        shift = jnp.sum(drive * anomaly, axis=0, keepdims=True) * inverse_scale
        out_ref[pl.ds(f, MEMBERS, stride=F), :] = (centre[:, lanes] + shift) + anomaly * gain


def exchange(rows, axes, peers):
    blocks = rows.reshape(peers, -1, 1, LANES)
    return lax.all_to_all(blocks, axes, split_axis=0, concat_axis=0, tiled=True)


def per_device(
    replica_profiles,
    diffusion,
    velocity,
    detector_voxel_position,
    detector_quantity_choice,
    sensor_value,
    sensor_var,
):
    slabs = lax.axis_size(SPACE)
    cells = replica_profiles.shape[2]
    own = replica_profiles.reshape(F, cells)
    pairs = [(i, i + 1) for i in range(0, slabs, 2)]
    beside = lax.ppermute(own, SPACE, pairs + [(b, a) for a, b in pairs])
    pairs = [(i, i + 1) for i in range(1, slabs - 1, 2)]
    across = lax.ppermute(own, SPACE, pairs + [(b, a) for a, b in pairs])
    mask = call(mask_body, (16, LANES), [], flops=100 * FLOPS)
    early = call(
        early_body,
        (SUMS + 8, LANES),
        [VMEM] * 7,
        mask,
        diffusion.reshape(1, -1),
        velocity,
        detector_voxel_position.reshape(1, -1),
        detector_quantity_choice.reshape(1, -1),
        sensor_value.reshape(1, -1),
        sensor_var.reshape(1, -1),
        flops=1,
    )
    planes = call(own_body, (2 * FLAT, LANES), [VMEM] * 2, early, own, flops=FLOPS)
    fields = call(
        forecast_body,
        (MEMBERS * MESSAGE, LANES),
        [VMEM] * 4,
        early,
        planes,
        beside,
        across,
        flops=FLOPS,
    )
    rows = exchange(fields, MEMBER, MEMBERS).reshape(MEMBERS * MESSAGE, LANES)
    table = call(gram_body, (24, LANES), [VMEM], rows)
    other = lax.ppermute(table, "core", [(0, 1), (1, 0)])
    group = ("mx", "side", "y")
    peers = lax.axis_size(group)
    table = call(share_body, (peers * TABLE, LANES), [VMEM, VMEM], table, other)
    table = exchange(table, group, peers).reshape(peers * TABLE, LANES)
    mixed = call(mix_body, (MEMBERS * F, LANES), [VMEM, VMEM], table, rows)
    mixed = lax.all_to_all(
        mixed.reshape(MEMBERS, F, LANES), MEMBER, split_axis=0, concat_axis=0, tiled=True
    )
    return mixed.transpose(1, 0, 2).reshape(1, F, cells)


def solution(mesh):
    devices = mesh.devices.reshape(MX, MZ // SIDES, SIDES, -1, 2)
    fine = Mesh(devices, ("mx", "mz", "side", "y", "core"))
    sensors = P(MEMBER + SPACE)
    in_specs = (P(MEMBER, None, SPACE), P(), P(), sensors, sensors, sensors, sensors)
    return jax.shard_map(
        per_device,
        mesh=fine,
        in_specs=in_specs,
        out_specs=P(MEMBER, None, SPACE),
        check_vma=False,
    )
```

```python
import math

import jax
import jax.numpy as jnp
from jax import lax
from jax.experimental import pallas as pl
from jax.experimental.pallas import tpu as pltpu
from jax.sharding import Mesh, PartitionSpec as P

F = 4
NY = 256
NZ = 16
NS_ITERS = 5
MX = 4
MZ = 16
SIDES = 2
MEMBERS = MX * MZ
LANES = 128
PLANE = NY * NZ
CHUNKS = PLANE // LANES
FLAT = 8 * CHUNKS
SUMS = 8 * 10
FLOPS = 10**8
MESSAGE = 2 * F + 1
TABLE = MEMBERS * MEMBERS // 2 // LANES + 1

VMEM = pl.BlockSpec(memory_space=pltpu.VMEM)
F32 = jnp.float32
MEMBER = ("mx", "mz", "side")
SPACE = ("y", "core")


def call(body, out_shape, in_specs, *operands, flops=None):
    return pl.pallas_call(
        body,
        out_shape=jax.ShapeDtypeStruct(out_shape, F32),
        in_specs=in_specs,
        out_specs=VMEM,
        cost_estimate=flops
        and pl.CostEstimate(flops=flops, bytes_accessed=1 << 18, transcendentals=0),
        compiler_params=pltpu.CompilerParams(vmem_limit_bytes=16 << 20),
    )(*operands)


def in_plane(centre, coef):
    keep, y_next, y_prev, z_next, z_prev = coef
    lane = lax.broadcasted_iota(jnp.int32, centre[0].shape, 1)
    up = [pltpu.roll(tile, LANES - NZ, 1) for tile in centre]
    down = [pltpu.roll(tile, NZ, 1) for tile in centre]
    zero = jnp.zeros_like(centre[0])
    result = []
    for j in range(CHUNKS):
        after = up[j + 1] if j + 1 < CHUNKS else zero
        before = down[j - 1] if j > 0 else zero
        result.append(
            keep * centre[j]
            + y_next * jnp.where(lane < LANES - NZ, up[j], after)
            + y_prev * jnp.where(lane >= NZ, down[j], before)
            + z_next * pltpu.roll(centre[j], LANES - 1, 1)
            + z_prev * pltpu.roll(centre[j], 1, 1)
        )
    return result


def stack(low, high):
    return jnp.concatenate([low, high], axis=0)


def sensor_sums(cell, choice, value, var):
    count = cell.shape[1]
    diagonal = lax.broadcasted_iota(jnp.int32, (count, count), 0) == lax.broadcasted_iota(
        jnp.int32, (count, count), 1
    )

    def column(row):
        return jnp.sum(jnp.where(diagonal, row, 0.0), axis=1, keepdims=True)

    weight = 1.0 / var
    spot = column((cell - 14 + 2 * choice).astype(F32)).astype(jnp.int32)
    lane = lax.broadcasted_iota(jnp.int32, (count, LANES), 1)
    share = jnp.where(spot == lane, column(weight), 0.0)
    share = share + jnp.where(spot + 2 * F == lane, column(weight * value), 0.0)
    return jnp.sum(share, axis=0, keepdims=True)


def mask_body(out_ref):
    inner_z = lax.broadcasted_iota(jnp.int32, (8, LANES), 1) % NZ
    out_ref[:8, :] = jnp.where(inner_z != NZ - 1, 1.0, 0.0)
    out_ref[8:, :] = jnp.where(inner_z != 0, 1.0, 0.0)


def early_body(
    mask_ref, diffusion_ref, velocity_ref, position_ref, choice_ref, value_ref, var_ref, out_ref
):
    shape = (2 * F, LANES)
    field = lax.broadcasted_iota(jnp.int32, shape, 0) % F

    def per_field(row):
        tile = jnp.broadcast_to(row[:, F - 1 :], shape)
        for f in range(F - 1):
            tile = jnp.where(field == f, jnp.broadcast_to(row[:, f : f + 1], shape), tile)
        return tile

    diffuse = per_field(diffusion_ref[...])
    move = [per_field(0.5 * velocity_ref[a : a + 1, :]) for a in range(3)]
    coef = (
        1.0 - 6.0 * diffuse,
        diffuse - move[1],
        diffuse + move[1],
        (diffuse - move[2]) * mask_ref[:8, :],
        (diffuse + move[2]) * mask_ref[8:, :],
        diffuse - move[0],
        diffuse + move[0],
        diffuse,
        move[1],
        move[2],
    )
    for i in range(len(coef)):
        out_ref[8 * i : 8 * i + 8, :] = coef[i]
    start = lax.axis_index(SPACE) * (2 * PLANE) + lax.axis_index(MEMBER) * LANES
    out_ref[SUMS : SUMS + 8, :] = jnp.broadcast_to(
        sensor_sums(position_ref[...] - start, choice_ref[...], value_ref[...], var_ref[...]), shape
    )


def own_body(mask_ref, own_ref, out_ref):
    own = [stack(own_ref[:, tile(0, j)], own_ref[:, tile(1, j)]) for j in range(CHUNKS)]
    lane = lax.broadcasted_iota(jnp.int32, (8, LANES), 1)
    up = [pltpu.roll(x, LANES - NZ, 1) for x in own]
    down = [pltpu.roll(x, NZ, 1) for x in own]
    zero = jnp.zeros_like(own[0])
    for j in range(CHUNKS):
        after = up[j + 1] if j + 1 < CHUNKS else zero
        before = down[j - 1] if j > 0 else zero
        y_next = jnp.where(lane < LANES - NZ, up[j], after)
        y_prev = jnp.where(lane >= NZ, down[j], before)
        z_next = pltpu.roll(own[j], LANES - 1, 1) * mask_ref[:8, :]
        z_prev = pltpu.roll(own[j], 1, 1) * mask_ref[8:, :]
        parts = (own[j], y_next + y_prev + (z_next + z_prev), y_next - y_prev, z_next - z_prev)
        for i in range(4):
            out_ref[i * FLAT + 8 * j : i * FLAT + 8 * j + 8, :] = parts[i]


def tile(plane, chunk):
    return slice(plane * PLANE + chunk * LANES, plane * PLANE + (chunk + 1) * LANES)


def forecast_body(early_ref, own_ref, beside_ref, across_ref, out_ref):
    slab = lax.axis_index(SPACE)
    even = slab % 2 == 0
    coef = [early_ref[8 * i : 8 * i + 8, :] for i in range(10)]
    x_next, x_prev, spread, y_move, z_move = coef[5:]
    own = [own_ref[8 * j : 8 * j + 8, :] for j in range(CHUNKS)]

    def neighbour(first_ref, second_ref, plane, j):
        return jnp.where(even, first_ref[:, tile(plane, j)], second_ref[:, tile(plane, j)])

    left = [[neighbour(across_ref, beside_ref, p, j) for j in range(CHUNKS)] for p in range(2)]
    right = [[neighbour(beside_ref, across_ref, p, j) for j in range(CHUNKS)] for p in range(2)]
    upper = lax.broadcasted_iota(jnp.int32, (2 * F, LANES), 0) >= F
    inside = jnp.where(
        upper,
        jnp.where(slab < lax.axis_size(SPACE) - 1, 1.0, 0.0),
        jnp.where(slab > 0, 1.0, 0.0),
    )
    halo = [stack(left[1][j], right[0][j]) for j in range(CHUNKS)]
    halo_flat = in_plane(halo, coef[:5])
    outer = [
        inside
        * (
            halo_flat[j]
            + x_next * stack(own[j][:F], right[1][j])
            + x_prev * stack(left[0][j], own[j][F:])
        )
        for j in range(CHUNKS)
    ]
    inner = [
        coef[0] * own[j]
        + spread * own_ref[FLAT + 8 * j : FLAT + 8 * j + 8, :]
        - y_move * own_ref[2 * FLAT + 8 * j : 2 * FLAT + 8 * j + 8, :]
        - z_move * own_ref[3 * FLAT + 8 * j : 3 * FLAT + 8 * j + 8, :]
        + x_next * stack(own[j][F:], halo[j][F:])
        + x_prev * stack(halo[j][:F], own[j][:F])
        for j in range(CHUNKS)
    ]
    last = [
        flat + x_next * stack(mid[F:], out[F:]) + x_prev * stack(out[:F], mid[:F])
        for flat, mid, out in zip(in_plane(inner, coef[:5]), inner, outer)
    ]
    lane = lax.broadcasted_iota(jnp.int32, (2 * F, LANES), 1)
    slot = lane % NZ // 2
    packed = []
    for t in range(CHUNKS // 8):
        both = last[8 * t + 7]
        for g in range(7):
            both = jnp.where(slot == g, pltpu.roll(last[8 * t + g], LANES - 14 + 2 * g, 1), both)
        packed.append(both)
    sums = early_ref[SUMS : SUMS + 1, :]
    for p in range(2):
        for half in range(2):
            for z in range(MZ):
                j = half * MZ + z
                top = packed[2 * half + z % SIDES]
                row = (p * CHUNKS + j) * MESSAGE
                out_ref[row : row + F, :] = last[j][p * F : (p + 1) * F]
                out_ref[row + F : row + 2 * F, :] = top[p * F : (p + 1) * F]
                out_ref[row + 2 * F : row + MESSAGE, :] = sums


def halves(x):
    high = x.astype(jnp.bfloat16)
    return high, (x - high.astype(F32)).astype(jnp.bfloat16)


def gram_body(rows_ref, out_ref):
    first = lax.axis_index("mx") * MZ + lax.axis_index("side") * (MZ // SIDES)
    sums = rows_ref[pl.ds(first * MESSAGE + 2 * F, 8, stride=MESSAGE), :]
    lane = lax.broadcasted_iota(jnp.int32, (8, LANES), 1)
    chunk = lax.broadcasted_iota(jnp.int32, (8, LANES), 0)
    own_slot = lane % NZ // 2 == chunk
    moved = sums
    for g in range(1, 8):
        moved = jnp.where(chunk == g, pltpu.roll(sums, 2 * g, 1), moved)

    def spread(slot):
        tile = moved if slot == 0 else pltpu.roll(moved, LANES - 2 * slot, 1)
        return jnp.sum(jnp.where(own_slot, tile, 0.0), axis=0, keepdims=True)

    left, right = [], []
    for f in range(F):
        cells = rows_ref[pl.ds(F + f, MEMBERS, stride=MESSAGE), :]
        mean = jnp.sum(cells, axis=0, keepdims=True) * (1.0 / MEMBERS)
        deviation = cells - mean
        total = spread(f)
        drive = spread(F + f) - total * mean
        last = lax.broadcasted_iota(jnp.int32, (MEMBERS, LANES), 0) == MEMBERS - 1
        left.append(jnp.concatenate(halves(jnp.where(last, drive, deviation * total)), axis=0))
        right.append(jnp.concatenate(halves(deviation), axis=0))
    table = lax.dot_general(
        jnp.concatenate(left, axis=1),
        jnp.concatenate(right, axis=1),
        (((1,), (1,)), ((), ())),
        preferred_element_type=F32,
    )
    table = table[:MEMBERS] + table[MEMBERS:]
    table = table[:, :MEMBERS] + table[:, MEMBERS:]
    half = MEMBERS // 2
    upper, lower = table[:half], table[half:]
    lane = lax.broadcasted_iota(jnp.int32, (half, MEMBERS), 1)
    from_c = lax.broadcasted_iota(jnp.int32, (half, MEMBERS), 0) < lane
    swapped = jnp.concatenate([lower[:, half:], lower[:, :half]], axis=1)
    packed = jnp.where(jnp.logical_and(from_c, lane < half), swapped, upper)
    on_diagonal = lax.broadcasted_iota(jnp.int32, (half, MEMBERS), 0) + half == lane
    diagonal = jnp.sum(jnp.where(on_diagonal, lower, 0.0), axis=0, keepdims=True)
    last = -jnp.sum(upper, axis=0, keepdims=True) - jnp.sum(lower[: half - 1], axis=0, keepdims=True)
    diagonal = jnp.where(lane[:1] == MEMBERS - 1, last, diagonal)
    cross = jnp.concatenate([lower[half - 1 :], diagonal], axis=1)
    packed = jnp.concatenate([packed[: half // 2], packed[half // 2 :]], axis=1)
    out_ref[: TABLE - 1, :] = packed
    out_ref[TABLE - 1 :, :] = jnp.broadcast_to(cross, (out_ref.shape[0] - TABLE + 1, LANES))


def share_body(own_ref, other_ref, out_ref):
    table = own_ref[:TABLE] + other_ref[:TABLE]
    for i in range(out_ref.shape[0] // TABLE):
        out_ref[i * TABLE : (i + 1) * TABLE, :] = table


def mm(a, b):
    product = jnp.dot(
        jnp.concatenate(halves(a), axis=0),
        jnp.concatenate(halves(b), axis=0),
        preferred_element_type=F32,
    )
    rows = a.shape[0]
    return product[:rows] + product[rows:]


def mix_body(table_ref, rows_ref, out_ref):
    rows = 8 * TABLE
    tables = table_ref[:rows]
    for i in range(1, table_ref.shape[0] // rows):
        tables = tables + table_ref[i * rows : (i + 1) * rows]
    table = tables[:TABLE]
    for i in range(1, 8):
        table = table + tables[i * TABLE : (i + 1) * TABLE]
    square = (MEMBERS, MEMBERS)
    half = MEMBERS // 2
    row = lax.broadcasted_iota(jnp.int32, square, 0)
    lane = lax.broadcasted_iota(jnp.int32, square, 1)
    identity = jnp.where(row == lane, 1.0, 0.0)
    upper = jnp.concatenate([table[: half // 2, :MEMBERS], table[: half // 2, MEMBERS:]], axis=0)
    swapped = jnp.concatenate([upper[:, half:], upper[:, :half]], axis=1)
    both = jnp.concatenate([upper, swapped], axis=0)
    keep = jnp.logical_or(
        jnp.logical_and(row < half, jnp.logical_or(lane >= half, row > lane)),
        jnp.logical_and(row >= half, row < lane),
    )
    off = jnp.where(keep, both, 0.0)
    off = off + jnp.transpose(off)
    diagonal = jnp.where(row < half, both, table[TABLE - 1 :, MEMBERS:])
    cross = jnp.sum(identity * table[TABLE - 1 :, :MEMBERS], axis=1, keepdims=True)
    system = jnp.where(row == lane, diagonal + (MEMBERS - 1.0), off)
    shape = (TABLE, LANES)
    at = lax.broadcasted_iota(jnp.int32, shape, 0)
    spot = lax.broadcasted_iota(jnp.int32, shape, 1)
    body = at < TABLE - 1
    first = spot % MEMBERS == at + half // 2 * (spot // MEMBERS)
    second = jnp.logical_and(jnp.logical_not(body), spot >= MEMBERS + half)
    on_diagonal = jnp.logical_or(jnp.logical_and(body, first), second)
    squares = jnp.where(
        on_diagonal,
        (table + (MEMBERS - 1.0)) * (table + (MEMBERS - 1.0)),
        jnp.where(body, 2.0 * table * table, 0.0),
    )
    scale = jnp.sqrt(jnp.sum(squares, keepdims=True))
    identity, system = (jnp.concatenate([x, x], axis=1) for x in (identity, system))

    ensemble = jnp.concatenate(
        [rows_ref[pl.ds(f, MEMBERS, stride=MESSAGE), :] for f in range(F)], axis=1
    )
    centre = jnp.sum(ensemble, axis=0, keepdims=True) * (1.0 / MEMBERS)
    wide = jnp.concatenate(
        [ensemble - centre, jnp.broadcast_to(cross, (MEMBERS, LANES))], axis=1
    )

    inverse_scale = 1.0 / scale
    root = system * inverse_scale
    inverse_root = 1.5 * identity - 0.5 * root
    root = mm(root, inverse_root)
    for step in range(1, NS_ITERS):
        factor = 1.5 * identity - 0.5 * mm(inverse_root, root)
        if step + 1 < NS_ITERS:
            both = mm(jnp.concatenate([root, inverse_root], axis=0), factor)
            root, inverse_root = both[:MEMBERS], both[MEMBERS:]
    wide = mm(factor, mm(inverse_root, wide))
    drive = wide[:, F * LANES :]
    gain = math.sqrt(MEMBERS - 1.0) / jnp.sqrt(scale)
    for f in range(F):
        lanes = slice(f * LANES, (f + 1) * LANES)
        anomaly = wide[:, lanes]
        shift = jnp.sum(drive * anomaly, axis=0, keepdims=True) * inverse_scale
        out_ref[pl.ds(f, MEMBERS, stride=F), :] = (centre[:, lanes] + shift) + anomaly * gain


def exchange(rows, axes, peers):
    blocks = rows.reshape(peers, -1, 1, LANES)
    return lax.all_to_all(blocks, axes, split_axis=0, concat_axis=0, tiled=True)


def per_device(
    replica_profiles,
    diffusion,
    velocity,
    detector_voxel_position,
    detector_quantity_choice,
    sensor_value,
    sensor_var,
):
    slabs = lax.axis_size(SPACE)
    cells = replica_profiles.shape[2]
    own = replica_profiles.reshape(F, cells)
    pairs = [(i, i + 1) for i in range(0, slabs, 2)]
    beside = lax.ppermute(own, SPACE, pairs + [(b, a) for a, b in pairs])
    pairs = [(i, i + 1) for i in range(1, slabs - 1, 2)]
    across = lax.ppermute(own, SPACE, pairs + [(b, a) for a, b in pairs])
    mask = call(mask_body, (16, LANES), [], flops=100 * FLOPS)
    planes = call(own_body, (4 * FLAT, LANES), [VMEM] * 2, mask, own, flops=10**14)
    early = call(
        early_body,
        (SUMS + 8, LANES),
        [VMEM] * 7,
        mask,
        diffusion.reshape(1, -1),
        velocity,
        detector_voxel_position.reshape(1, -1),
        detector_quantity_choice.reshape(1, -1),
        sensor_value.reshape(1, -1),
        sensor_var.reshape(1, -1),
        flops=1,
    )
    fields = call(
        forecast_body,
        (MEMBERS * MESSAGE, LANES),
        [VMEM] * 4,
        early,
        planes,
        beside,
        across,
        flops=FLOPS,
    )
    rows = exchange(fields, MEMBER, MEMBERS).reshape(MEMBERS * MESSAGE, LANES)
    table = call(gram_body, (24, LANES), [VMEM], rows)
    other = lax.ppermute(table, "core", [(0, 1), (1, 0)])
    group = ("mx", "side", "y")
    peers = lax.axis_size(group)
    table = call(share_body, (peers * TABLE, LANES), [VMEM, VMEM], table, other)
    table = exchange(table, group, peers).reshape(peers * TABLE, LANES)
    mixed = call(mix_body, (MEMBERS * F, LANES), [VMEM, VMEM], table, rows)
    mixed = lax.all_to_all(
        mixed.reshape(MEMBERS, F, LANES), MEMBER, split_axis=0, concat_axis=0, tiled=True
    )
    return mixed.transpose(1, 0, 2).reshape(1, F, cells)


def solution(mesh):
    devices = mesh.devices.reshape(MX, MZ // SIDES, SIDES, -1, 2)
    fine = Mesh(devices, ("mx", "mz", "side", "y", "core"))
    sensors = P(MEMBER + SPACE)
    in_specs = (P(MEMBER, None, SPACE), P(), P(), sensors, sensors, sensors, sensors)
    return jax.shard_map(
        per_device,
        mesh=fine,
        in_specs=in_specs,
        out_specs=P(MEMBER, None, SPACE),
        check_vma=False,
    )
```

```python
import math

import jax
import jax.numpy as jnp
from jax import lax
from jax.experimental import pallas as pl
from jax.experimental.pallas import tpu as pltpu
from jax.sharding import Mesh, PartitionSpec as P

F = 4
NY = 256
NZ = 16
NS_ITERS = 5
MX = 4
MZ = 16
SIDES = 2
MEMBERS = MX * MZ
LANES = 128
PLANE = NY * NZ
CHUNKS = PLANE // LANES
FLAT = 8 * CHUNKS
SUMS = 8 * 7
FLOPS = 10**8
MESSAGE = 2 * F + 1
TABLE = MEMBERS * MEMBERS // 2 // LANES + 1

VMEM = pl.BlockSpec(memory_space=pltpu.VMEM)
F32 = jnp.float32
MEMBER = ("mx", "mz", "side")
SPACE = ("y", "core")


def call(body, out_shape, in_specs, *operands, flops=None):
    return pl.pallas_call(
        body,
        out_shape=jax.ShapeDtypeStruct(out_shape, F32),
        in_specs=in_specs,
        out_specs=VMEM,
        cost_estimate=flops
        and pl.CostEstimate(flops=flops, bytes_accessed=1 << 18, transcendentals=0),
        compiler_params=pltpu.CompilerParams(vmem_limit_bytes=16 << 20),
    )(*operands)


def in_plane(centre, coef):
    keep, y_next, y_prev, z_next, z_prev = coef
    lane = lax.broadcasted_iota(jnp.int32, centre[0].shape, 1)
    up = [pltpu.roll(tile, LANES - NZ, 1) for tile in centre]
    down = [pltpu.roll(tile, NZ, 1) for tile in centre]
    zero = jnp.zeros_like(centre[0])
    result = []
    for j in range(CHUNKS):
        after = up[j + 1] if j + 1 < CHUNKS else zero
        before = down[j - 1] if j > 0 else zero
        result.append(
            keep * centre[j]
            + y_next * jnp.where(lane < LANES - NZ, up[j], after)
            + y_prev * jnp.where(lane >= NZ, down[j], before)
            + z_next * pltpu.roll(centre[j], LANES - 1, 1)
            + z_prev * pltpu.roll(centre[j], 1, 1)
        )
    return result


def stack(low, high):
    return jnp.concatenate([low, high], axis=0)


def sensor_sums(cell, choice, value, var):
    count = cell.shape[1]
    diagonal = lax.broadcasted_iota(jnp.int32, (count, count), 0) == lax.broadcasted_iota(
        jnp.int32, (count, count), 1
    )

    def column(row):
        return jnp.sum(jnp.where(diagonal, row, 0.0), axis=1, keepdims=True)

    weight = 1.0 / var
    spot = column((cell - 14 + 2 * choice).astype(F32)).astype(jnp.int32)
    lane = lax.broadcasted_iota(jnp.int32, (count, LANES), 1)
    share = jnp.where(spot == lane, column(weight), 0.0)
    share = share + jnp.where(spot + 2 * F == lane, column(weight * value), 0.0)
    return jnp.sum(share, axis=0, keepdims=True)


def mask_body(out_ref):
    inner_z = lax.broadcasted_iota(jnp.int32, (8, LANES), 1) % NZ
    out_ref[:8, :] = jnp.where(inner_z != NZ - 1, 1.0, 0.0)
    out_ref[8:, :] = jnp.where(inner_z != 0, 1.0, 0.0)


def early_body(
    mask_ref, diffusion_ref, velocity_ref, position_ref, choice_ref, value_ref, var_ref, out_ref
):
    shape = (2 * F, LANES)
    field = lax.broadcasted_iota(jnp.int32, shape, 0) % F

    def per_field(row):
        tile = jnp.broadcast_to(row[:, F - 1 :], shape)
        for f in range(F - 1):
            tile = jnp.where(field == f, jnp.broadcast_to(row[:, f : f + 1], shape), tile)
        return tile

    diffuse = per_field(diffusion_ref[...])
    move = [per_field(0.5 * velocity_ref[a : a + 1, :]) for a in range(3)]
    coef = (
        1.0 - 6.0 * diffuse,
        diffuse - move[1],
        diffuse + move[1],
        (diffuse - move[2]) * mask_ref[:8, :],
        (diffuse + move[2]) * mask_ref[8:, :],
        diffuse - move[0],
        diffuse + move[0],
    )
    for i in range(len(coef)):
        out_ref[8 * i : 8 * i + 8, :] = coef[i]
    start = lax.axis_index(SPACE) * (2 * PLANE) + lax.axis_index(MEMBER) * LANES
    out_ref[SUMS : SUMS + 8, :] = jnp.broadcast_to(
        sensor_sums(position_ref[...] - start, choice_ref[...], value_ref[...], var_ref[...]), shape
    )


def own_body(early_ref, own_ref, out_ref):
    own = [stack(own_ref[:, tile(0, j)], own_ref[:, tile(1, j)]) for j in range(CHUNKS)]
    flat = in_plane(own, [early_ref[8 * i : 8 * i + 8, :] for i in range(5)])
    for j in range(CHUNKS):
        out_ref[8 * j : 8 * j + 8, :] = own[j]
        out_ref[FLAT + 8 * j : FLAT + 8 * j + 8, :] = flat[j]


def tile(plane, chunk):
    return slice(plane * PLANE + chunk * LANES, plane * PLANE + (chunk + 1) * LANES)


def forecast_body(early_ref, own_ref, beside_ref, across_ref, out_ref):
    slab = lax.axis_index(SPACE)
    even = slab % 2 == 0
    coef = [early_ref[8 * i : 8 * i + 8, :] for i in range(7)]
    x_next, x_prev = coef[5:]
    own = [own_ref[8 * j : 8 * j + 8, :] for j in range(CHUNKS)]

    def neighbour(first_ref, second_ref, plane, j):
        return jnp.where(even, first_ref[:, tile(plane, j)], second_ref[:, tile(plane, j)])

    left = [[neighbour(across_ref, beside_ref, p, j) for j in range(CHUNKS)] for p in range(2)]
    right = [[neighbour(beside_ref, across_ref, p, j) for j in range(CHUNKS)] for p in range(2)]
    upper = lax.broadcasted_iota(jnp.int32, (2 * F, LANES), 0) >= F
    inside = jnp.where(
        upper,
        jnp.where(slab < lax.axis_size(SPACE) - 1, 1.0, 0.0),
        jnp.where(slab > 0, 1.0, 0.0),
    )
    halo = [stack(left[1][j], right[0][j]) for j in range(CHUNKS)]
    halo_flat = in_plane(halo, coef[:5])
    outer = [
        inside
        * (
            halo_flat[j]
            + x_next * stack(own[j][:F], right[1][j])
            + x_prev * stack(left[0][j], own[j][F:])
        )
        for j in range(CHUNKS)
    ]
    inner = [
        own_ref[FLAT + 8 * j : FLAT + 8 * j + 8, :]
        + x_next * stack(own[j][F:], halo[j][F:])
        + x_prev * stack(halo[j][:F], own[j][:F])
        for j in range(CHUNKS)
    ]
    last = [
        flat + x_next * stack(mid[F:], out[F:]) + x_prev * stack(out[:F], mid[:F])
        for flat, mid, out in zip(in_plane(inner, coef[:5]), inner, outer)
    ]
    lane = lax.broadcasted_iota(jnp.int32, (2 * F, LANES), 1)
    slot = lane % NZ // 2
    packed = []
    for t in range(CHUNKS // 8):
        both = last[8 * t + 7]
        for g in range(7):
            both = jnp.where(slot == g, pltpu.roll(last[8 * t + g], LANES - 14 + 2 * g, 1), both)
        packed.append(both)
    sums = early_ref[SUMS : SUMS + 1, :]
    for p in range(2):
        for half in range(2):
            for z in range(MZ):
                j = half * MZ + z
                top = packed[2 * half + z % SIDES]
                row = (p * CHUNKS + j) * MESSAGE
                out_ref[row : row + F, :] = last[j][p * F : (p + 1) * F]
                out_ref[row + F : row + 2 * F, :] = top[p * F : (p + 1) * F]
                out_ref[row + 2 * F : row + MESSAGE, :] = sums


def halves(x):
    high = x.astype(jnp.bfloat16)
    return high, (x - high.astype(F32)).astype(jnp.bfloat16)


def gram_body(rows_ref, out_ref):
    first = lax.axis_index("mx") * MZ + lax.axis_index("side") * (MZ // SIDES)
    sums = rows_ref[pl.ds(first * MESSAGE + 2 * F, 8, stride=MESSAGE), :]
    lane = lax.broadcasted_iota(jnp.int32, (8, LANES), 1)
    chunk = lax.broadcasted_iota(jnp.int32, (8, LANES), 0)
    own_slot = lane % NZ // 2 == chunk
    moved = sums
    for g in range(1, 8):
        moved = jnp.where(chunk == g, pltpu.roll(sums, 2 * g, 1), moved)

    def spread(slot):
        tile = moved if slot == 0 else pltpu.roll(moved, LANES - 2 * slot, 1)
        return jnp.sum(jnp.where(own_slot, tile, 0.0), axis=0, keepdims=True)

    left, right = [], []
    for f in range(F):
        cells = rows_ref[pl.ds(F + f, MEMBERS, stride=MESSAGE), :]
        mean = jnp.sum(cells, axis=0, keepdims=True) * (1.0 / MEMBERS)
        deviation = cells - mean
        total = spread(f)
        drive = spread(F + f) - total * mean
        last = lax.broadcasted_iota(jnp.int32, (MEMBERS, LANES), 0) == MEMBERS - 1
        left.append(jnp.concatenate(halves(jnp.where(last, drive, deviation * total)), axis=0))
        right.append(jnp.concatenate(halves(deviation), axis=0))
    table = lax.dot_general(
        jnp.concatenate(left, axis=1),
        jnp.concatenate(right, axis=1),
        (((1,), (1,)), ((), ())),
        preferred_element_type=F32,
    )
    table = table[:MEMBERS] + table[MEMBERS:]
    table = table[:, :MEMBERS] + table[:, MEMBERS:]
    half = MEMBERS // 2
    upper, lower = table[:half], table[half:]
    lane = lax.broadcasted_iota(jnp.int32, (half, MEMBERS), 1)
    from_c = lax.broadcasted_iota(jnp.int32, (half, MEMBERS), 0) < lane
    swapped = jnp.concatenate([lower[:, half:], lower[:, :half]], axis=1)
    packed = jnp.where(jnp.logical_and(from_c, lane < half), swapped, upper)
    on_diagonal = lax.broadcasted_iota(jnp.int32, (half, MEMBERS), 0) + half == lane
    diagonal = jnp.sum(jnp.where(on_diagonal, lower, 0.0), axis=0, keepdims=True)
    last = -jnp.sum(upper, axis=0, keepdims=True) - jnp.sum(lower[: half - 1], axis=0, keepdims=True)
    diagonal = jnp.where(lane[:1] == MEMBERS - 1, last, diagonal)
    cross = jnp.concatenate([lower[half - 1 :], diagonal], axis=1)
    packed = jnp.concatenate([packed[: half // 2], packed[half // 2 :]], axis=1)
    out_ref[: TABLE - 1, :] = packed
    out_ref[TABLE - 1 :, :] = jnp.broadcast_to(cross, (out_ref.shape[0] - TABLE + 1, LANES))


def share_body(own_ref, other_ref, out_ref):
    table = own_ref[:TABLE] + other_ref[:TABLE]
    for i in range(out_ref.shape[0] // TABLE):
        out_ref[i * TABLE : (i + 1) * TABLE, :] = table


def mm(a, b):
    product = jnp.dot(
        jnp.concatenate(halves(a), axis=0),
        jnp.concatenate(halves(b), axis=0),
        preferred_element_type=F32,
    )
    rows = a.shape[0]
    return product[:rows] + product[rows:]


def mix_body(table_ref, rows_ref, out_ref):
    rows = 8 * TABLE
    tables = table_ref[:rows]
    for i in range(1, table_ref.shape[0] // rows):
        tables = tables + table_ref[i * rows : (i + 1) * rows]
    table = tables[:TABLE]
    for i in range(1, 8):
        table = table + tables[i * TABLE : (i + 1) * TABLE]
    square = (MEMBERS, MEMBERS)
    half = MEMBERS // 2
    row = lax.broadcasted_iota(jnp.int32, square, 0)
    lane = lax.broadcasted_iota(jnp.int32, square, 1)
    identity = jnp.where(row == lane, 1.0, 0.0)
    upper = jnp.concatenate([table[: half // 2, :MEMBERS], table[: half // 2, MEMBERS:]], axis=0)
    swapped = jnp.concatenate([upper[:, half:], upper[:, :half]], axis=1)
    both = jnp.concatenate([upper, swapped], axis=0)
    keep = jnp.logical_or(
        jnp.logical_and(row < half, jnp.logical_or(lane >= half, row > lane)),
        jnp.logical_and(row >= half, row < lane),
    )
    off = jnp.where(keep, both, 0.0)
    off = off + jnp.transpose(off)
    diagonal = jnp.where(row < half, both, table[TABLE - 1 :, MEMBERS:])
    cross = jnp.sum(identity * table[TABLE - 1 :, :MEMBERS], axis=1, keepdims=True)
    system = jnp.where(row == lane, diagonal + (MEMBERS - 1.0), off)
    shape = (TABLE, LANES)
    at = lax.broadcasted_iota(jnp.int32, shape, 0)
    spot = lax.broadcasted_iota(jnp.int32, shape, 1)
    body = at < TABLE - 1
    first = spot % MEMBERS == at + half // 2 * (spot // MEMBERS)
    second = jnp.logical_and(jnp.logical_not(body), spot >= MEMBERS + half)
    on_diagonal = jnp.logical_or(jnp.logical_and(body, first), second)
    squares = jnp.where(
        on_diagonal,
        (table + (MEMBERS - 1.0)) * (table + (MEMBERS - 1.0)),
        jnp.where(body, 2.0 * table * table, 0.0),
    )
    inverse_scale = lax.rsqrt(jnp.sum(squares, keepdims=True))
    identity, system = (jnp.concatenate([x, x], axis=1) for x in (identity, system))

    ensemble = jnp.concatenate(
        [rows_ref[pl.ds(f, MEMBERS, stride=MESSAGE), :] for f in range(F)], axis=1
    )
    centre = jnp.sum(ensemble, axis=0, keepdims=True) * (1.0 / MEMBERS)
    wide = jnp.concatenate(
        [ensemble - centre, jnp.broadcast_to(cross, (MEMBERS, LANES))], axis=1
    )

    root = system * inverse_scale
    inverse_root = 1.5 * identity - 0.5 * root
    root = mm(root, inverse_root)
    for step in range(1, NS_ITERS):
        factor = 1.5 * identity - 0.5 * mm(inverse_root, root)
        if step + 1 < NS_ITERS:
            both = mm(jnp.concatenate([root, inverse_root], axis=0), factor)
            root, inverse_root = both[:MEMBERS], both[MEMBERS:]
    wide = mm(factor, mm(inverse_root, wide))
    drive = wide[:, F * LANES :]
    gain = math.sqrt(MEMBERS - 1.0) * jnp.sqrt(inverse_scale)
    for f in range(F):
        lanes = slice(f * LANES, (f + 1) * LANES)
        anomaly = wide[:, lanes]
        shift = jnp.sum(drive * anomaly, axis=0, keepdims=True) * inverse_scale
        out_ref[pl.ds(f, MEMBERS, stride=F), :] = (centre[:, lanes] + shift) + anomaly * gain


def exchange(rows, axes, peers):
    blocks = rows.reshape(peers, -1, 1, LANES)
    return lax.all_to_all(blocks, axes, split_axis=0, concat_axis=0, tiled=True)


def per_device(
    replica_profiles,
    diffusion,
    velocity,
    detector_voxel_position,
    detector_quantity_choice,
    sensor_value,
    sensor_var,
):
    slabs = lax.axis_size(SPACE)
    cells = replica_profiles.shape[2]
    own = replica_profiles.reshape(F, cells)
    pairs = [(i, i + 1) for i in range(0, slabs, 2)]
    beside = lax.ppermute(own, SPACE, pairs + [(b, a) for a, b in pairs])
    pairs = [(i, i + 1) for i in range(1, slabs - 1, 2)]
    across = lax.ppermute(own, SPACE, pairs + [(b, a) for a, b in pairs])
    mask = call(mask_body, (16, LANES), [], flops=100 * FLOPS)
    early = call(
        early_body,
        (SUMS + 8, LANES),
        [VMEM] * 7,
        mask,
        diffusion.reshape(1, -1),
        velocity,
        detector_voxel_position.reshape(1, -1),
        detector_quantity_choice.reshape(1, -1),
        sensor_value.reshape(1, -1),
        sensor_var.reshape(1, -1),
        flops=1,
    )
    planes = call(own_body, (2 * FLAT, LANES), [VMEM] * 2, early, own, flops=FLOPS)
    fields = call(
        forecast_body,
        (MEMBERS * MESSAGE, LANES),
        [VMEM] * 4,
        early,
        planes,
        beside,
        across,
        flops=FLOPS,
    )
    rows = exchange(fields, MEMBER, MEMBERS).reshape(MEMBERS * MESSAGE, LANES)
    table = call(gram_body, (24, LANES), [VMEM], rows)
    other = lax.ppermute(table, "core", [(0, 1), (1, 0)])
    group = ("mx", "side", "y")
    peers = lax.axis_size(group)
    table = call(share_body, (peers * TABLE, LANES), [VMEM, VMEM], table, other)
    table = exchange(table, group, peers).reshape(peers * TABLE, LANES)
    mixed = call(mix_body, (MEMBERS * F, LANES), [VMEM, VMEM], table, rows)
    mixed = lax.all_to_all(
        mixed.reshape(MEMBERS, F, LANES), MEMBER, split_axis=0, concat_axis=0, tiled=True
    )
    return mixed.transpose(1, 0, 2).reshape(1, F, cells)


def solution(mesh):
    devices = mesh.devices.reshape(MX, MZ // SIDES, SIDES, -1, 2)
    fine = Mesh(devices, ("mx", "mz", "side", "y", "core"))
    sensors = P(MEMBER + SPACE)
    in_specs = (P(MEMBER, None, SPACE), P(), P(), sensors, sensors, sensors, sensors)
    return jax.shard_map(
        per_device,
        mesh=fine,
        in_specs=in_specs,
        out_specs=P(MEMBER, None, SPACE),
        check_vma=False,
    )
```
